128 devices in a mesh: scen: 16 (over y, x), veh: 8 (over z, core).
Axes of the slice: x: 4, y: 4, z: 4, core: 2. Of those that a mesh axis runs over, the one named last changes fastest.
Arguments:
- start_plan: bfloat16 [256, 7168, 128], P('scen', 'veh'), may hold values from -6 to 6
- linear_cost: bfloat16 [256, 7168, 128], P('scen', 'veh'), may hold values from -12 to 12
- price: bfloat16 [256, 7168, 128], P('scen', 'veh'), may hold values from -6 to 6
- anchor: bfloat16 [16, 7168, 128], P(None, 'veh'), may hold values from -6 to 6
- hessian: bfloat16 [256, 128, 128], P('scen'), as said below
- usage_coef: bfloat16 [7168, 128], P('veh'), may hold values from -1.5 to 1.5
- crew_limit: float32 [256, 350], P('scen'), may hold values from -48 to 48
- crew_dual: float32 [256, 350], P('scen'), may hold values from 0 to 2
- crew_row: int32 [7168], P('veh'), may hold values from 0 to 349
- bundle_of: int32 [256, 1], replicated, may hold values from 0 to 15
- scen_weight: int32 [256], replicated, may hold values from 1 to 8
Outputs:
- new_plan: bfloat16 [256, 7168, 128], P('scen', 'veh')
- new_price: bfloat16 [256, 7168, 128], P('scen', 'veh')
- bundle_mean: bfloat16 [16, 7168, 128], P('scen', 'veh')
- new_dual: float32 [256, 350], P('scen')
- gap: float32 [], replicated
The draws below stay inside these ranges and needn't reach their ends.
Inputs may be any that keep to these rules, and one draw needn't show every extreme that they name: `bundle_of`: every bundle holds one scenario or more. `hessian`: symmetric.
All inputs are finite; a program needn't handle non-finite values.
Results may differ from the reference program's by a relative error of at most 0.0013.
The reference program's roundings to bfloat16 on the way (of `rounded`) count: a program that leaves them out, or rounds other values in their place, can miss the bound.
Values sent between devices are 32-bit elements; how exact they have to be, the bound alone decides.
No kernel may reach another device: no remote copies, remote signals or barrier semaphores. Data moves between devices by JAX's collectives and lax.ppermute only.
A program may use at most 128 MiB of HBM per device.

```python
import jax
import jax.numpy as jnp
from jax import lax

NV = 128
CREW = 350
ITERS = 12
S = 256
NB = 16
V = 7168


def draw_hessian(key, part):
    key_off, key_diag = jax.random.split(key)
    raw_values = jax.random.uniform(key_off, (S, NV, NV), jnp.float32, -1.0, 1.0)
    limit_value = 3.8 / (NV - 1)
    symmetric = 0.5 * limit_value * (raw_values + jnp.swapaxes(raw_values, 1, 2))
    identity = jnp.eye(NV, dtype=jnp.float32)
    diagonal = jax.random.uniform(key_diag, (S, 1, NV), jnp.float32, 1.0, 3.0) + 3.8
    return (symmetric * (1.0 - identity) + identity * diagonal).astype(jnp.bfloat16)


def plant(drawn, key, smallest, largest):
    longest = drawn.shape.index(max(drawn.shape))
    spots = []
    for shift in (0, 1):
        where = [jax.random.randint(jax.random.fold_in(key, axis), (), 0, length) for axis, length in enumerate(drawn.shape)]
        where[longest] = (where[longest] + shift) % drawn.shape[longest]
        spots.append(tuple(where))
    return drawn.at[spots[0]].set(smallest).at[spots[1]].set(largest)


def block_levels(own_key, dims, cuts, least, high):
    level, own = 1.0, jax.random.fold_in(own_key, 6)
    for position, parts in cuts:
        heights = jnp.exp(jax.random.uniform(jax.random.fold_in(own, position), (parts,), jnp.float32, least / len(cuts), high / len(cuts)))
        level = level * jnp.repeat(heights, dims[position] // parts).reshape([-1 if axis == position else 1 for axis in range(len(dims))])
    return level


def distinct(key, rows, count, top, lift):
    ranking = jax.random.permutation(jax.random.fold_in(key, 1), count)
    boost = ranking
    for power in range(3):
        boost = boost * boost // count
    boost = boost * lift // count
    lots = jax.random.randint(jax.random.fold_in(key, 2), (rows, count), 0, 4096) + boost
    holders = jax.random.permutation(jax.random.fold_in(key, 3), rows)[jnp.arange(count) % rows]
    lots = jnp.where(jnp.arange(rows)[:, None] == holders[None, :], 1 << 14, lots)
    score = lots * count + jnp.arange(count)
    return lax.top_k(score.astype(jnp.int32), top)[1].astype(jnp.int32)


def centred(stream_key, dims, scale, reach, pieces=(), kind=jnp.bfloat16):
    array = jax.random.normal(stream_key, dims, jnp.float32) * scale
    if len(pieces) > 0:
        array = block_levels(stream_key, dims, pieces, -0.22, 0.18) * array
    return jnp.clip(array, min=-reach, max=reach).astype(kind)


def setup_inputs(seed: int = 0) -> dict:
    keys = jax.random.split(jax.random.key(seed), 12)
    return {
        "start_plan": centred(keys[0], (S, V, NV), 1.0, 6.0, ((0, 16), (1, 8))),
        "linear_cost": centred(keys[1], (S, V, NV), 2.0, 12.0, ((0, 16), (1, 8))),
        "price": centred(keys[2], (S, V, NV), 1.0, 6.0, ((0, 16), (1, 8))),
        "anchor": centred(keys[3], (NB, V, NV), 1.0, 6.0, ((1, 8),)),
        "hessian": draw_hessian(jax.random.fold_in(keys[11], 71), 0),
        "usage_coef": centred(keys[5], (V, NV), 0.25, 1.5, ((0, 8),)),
        "crew_limit": centred(keys[6], (S, CREW), 8.0, 48.0, ((0, 16),), jnp.float32),
        "crew_dual": jnp.clip(2.0 * jax.random.uniform(keys[7], (S, CREW), jnp.float32) ** block_levels(keys[7], (S, CREW), ((0, 16),), -0.2, 0.2), 0.0, 2.0),
        "crew_row": plant(jax.random.randint(keys[8], (V,), 0, CREW), jax.random.fold_in(keys[8], 1), 0, CREW - 1).astype(jnp.int32),
        "bundle_of": distinct(keys[9], S, NB, 1, 1024),
        "scen_weight": plant(jax.random.randint(keys[10], (S,), 1, 9), jax.random.fold_in(keys[10], 1), 1, 8).astype(jnp.int32),
    }


penalty = 1.0
step_size = 0.02
dual_step = 0.02
highest = lax.Precision.HIGHEST

def reference(start_plan, linear_cost, price, anchor, hessian, usage_coef, crew_limit, crew_dual, crew_row, bundle_of, scen_weight):
    bundles = bundle_of[:, 0]
    weights = scen_weight.astype(jnp.float32)
    coefficient = usage_coef.astype(jnp.float32)
    crew_map = (crew_row[:, None] == jnp.arange(CREW, dtype=jnp.int32)[None, :]).astype(jnp.float32)

    def solve_one(inputs):
        start_one, cost_one, price_one, bundle_one, hess_one, limit_one, dual_one = inputs
        anchored = lax.dynamic_index_in_dim(anchor, bundle_one, 0, keepdims=False).astype(jnp.float32)
        linear_part = cost_one.astype(jnp.float32) + price_one.astype(jnp.float32) - penalty * anchored
        hess_wide = hess_one.astype(jnp.float32)

        def advance(index, state_pair):
            roster, multiplier = state_pair
            rounded = lax.optimization_barrier(roster.astype(jnp.bfloat16)).astype(jnp.float32)
            curvature = jnp.dot(rounded, hess_wide, precision=highest)
            consumed = lax.optimization_barrier(jnp.sum(roster * coefficient, axis=1))
            usage = jnp.dot(consumed, crew_map, precision=highest)
            updated = jnp.maximum(multiplier + dual_step * (usage - limit_one), 0.0)
            per_vehicle = jnp.dot(crew_map, multiplier, precision=highest)
            gradient = curvature + linear_part + penalty * roster + per_vehicle[:, None] * coefficient
            return (roster - step_size * gradient, updated)
        return lax.fori_loop(0, ITERS, advance, (start_one.astype(jnp.float32), dual_one))
    roster, multiplier = lax.map(solve_one, (start_plan, linear_cost, price, bundles, hessian, crew_limit, crew_dual))
    selector = (bundles[:, None] == jnp.arange(NB, dtype=jnp.int32)[None, :]).astype(jnp.float32)
    bundle_weight = lax.optimization_barrier(jnp.sum(selector * weights[:, None], axis=0))
    totals = jnp.einsum('sb,svi->bvi', selector * weights[:, None], roster, precision=highest)
    mean_all = totals / bundle_weight[:, None, None]
    mean_here = jnp.einsum('sb,bvi->svi', selector, mean_all, precision=highest)
    deviation = roster - mean_here
    new_price = (price.astype(jnp.float32) + penalty * deviation).astype(jnp.bfloat16)
    spread = jnp.sum(weights * lax.optimization_barrier(jnp.sum(deviation * deviation, axis=(1, 2))))
    gap = jnp.sqrt(spread / (jnp.sum(weights) * V * NV))
    return (roster.astype(jnp.bfloat16), new_price, mean_all.astype(jnp.bfloat16), multiplier, gap)
```

```python
import functools

import jax
import jax.numpy as jnp
from jax import lax
from jax.experimental import pallas as pl
from jax.experimental.pallas import tpu as pltpu
from jax.sharding import PartitionSpec as P

ITERS = 12
penalty = 1.0
step_size = 0.02
dual_step = 0.02
keep = 1.0 - step_size * penalty
CREW_PAD = 384
LIMIT = 56 * 1024 * 1024
bf16 = jnp.bfloat16
f32 = jnp.float32

PAIR_A = {0: 1, 1: 0, 2: 3, 3: 2}
PAIR_B = {0: 3, 3: 0, 1: 2, 2: 1}


def split3(value):
    hi = value.astype(bf16)
    rest = value - hi.astype(f32)
    mid = rest.astype(bf16)
    low = (rest - mid.astype(f32)).astype(bf16)
    return jnp.concatenate([hi, mid, low], axis=0)


def exact_dot(left, right):
    rows = left.shape[0]
    out = jnp.dot(split3(left), right, preferred_element_type=f32)
    return out[:rows] + out[rows : 2 * rows] + out[2 * rows :]


def folded(value):
    return jnp.sum(value.reshape(-1, 8, value.shape[1]), axis=0)


def lane_chunks(width):
    chunks, start = [], 0
    while start < width:
        size = min(256, width - start)
        chunks.append(pl.ds(start, size))
        start += size
    return chunks


def first_kernel(
    bundles,
    start_ref,
    cost_ref,
    price_ref,
    anchor_ref,
    hess_ref,
    coef_ref,
    dual_ref,
    row_to_veh,
    veh_to_row,
    partial_ref,
    linear_ref,
    coef_t_ref,
    usage_ref,
    crew_scr,
    used_scr,
):
    s = pl.program_id(0)
    count = pl.num_programs(0)
    n = hess_ref.shape[-1]
    eye = (
        lax.broadcasted_iota(jnp.int32, (n, n), 0) == lax.broadcasted_iota(jnp.int32, (n, n), 1)
    ).astype(bf16)

    def turned(block):
        return lax.dot_general(eye, block, (((1,), (1,)), ((), ())), preferred_element_type=f32)

    @pl.when(s == 0)
    def _():
        crew_scr[:, 0, :] = step_size * exact_dot(dual_ref[...], row_to_veh[...])
        used_scr[...] = jnp.zeros_like(used_scr)
        for cols in lane_chunks(used_scr.shape[2]):
            c = turned(coef_ref[cols, :])
            coef_t_ref[:, cols] = c
            used_scr[48, :, cols] = folded(c * c)

    hess = hess_ref[0]
    for cols in lane_chunks(used_scr.shape[2]):
        c = coef_t_ref[:, cols]
        linear = step_size * (
            turned(cost_ref[0, cols, :])
            + turned(price_ref[0, cols, :])
            - penalty * turned(anchor_ref[0, cols, :])
        )
        linear_ref[0, :, cols] = linear
        x = turned(start_ref[0, cols, :])
        used_scr[s, :, cols] = folded(c * x)
        curve = jnp.dot(hess, x.astype(bf16), preferred_element_type=f32)
        x = (keep * x - linear) - step_size * curve - crew_scr[s, :, cols] * c
        used_scr[16 + s, :, cols] = folded(c * x)
        curve = jnp.dot(hess, x.astype(bf16), preferred_element_type=f32)
        x = (keep * x - linear) - step_size * curve
        used_scr[32 + s, :, cols] = folded(c * x)
        partial_ref[0, :, cols] = x

    @pl.when(s == count - 1)
    def _():
        usage_ref[...] = exact_dot(jnp.sum(used_scr[...], axis=1), veh_to_row[...])


def crew_update(usage, norms, limit, dual):
    one = jnp.maximum(dual + dual_step * (usage[0:16] - limit), 0.0)
    third = usage[32:48] - step_size * one * norms
    two = jnp.maximum(one + dual_step * (usage[16:32] - limit), 0.0)
    three = jnp.maximum(two + dual_step * (third - limit), 0.0)
    return one, two, three


def middle_kernel(
    partial_ref,
    linear_ref,
    hess_ref,
    coef_t_ref,
    use_a,
    use_b,
    norms_ref,
    limit_ref,
    dual_ref,
    row_to_veh,
    veh_to_row,
    next_ref,
    usage_ref,
    new_dual_ref,
    crew_scr,
    used_scr,
):
    s = pl.program_id(0)
    count = pl.num_programs(0)

    @pl.when(s == 0)
    def _():
        one, two, three = crew_update(
            use_a[0:48] + use_b[0:48], norms_ref[0:1], limit_ref[...], dual_ref[...]
        )
        new_dual_ref[...] = three
        crew_scr[:, 0, :] = step_size * exact_dot(
            jnp.concatenate([one, two, three], axis=0), row_to_veh[...]
        )

    hess = hess_ref[0]
    for cols in lane_chunks(used_scr.shape[2]):
        c = coef_t_ref[:, cols]
        linear = linear_ref[0, :, cols]
        x = partial_ref[0, :, cols] - crew_scr[s, :, cols] * c
        for k in (1, 2):
            curve = jnp.dot(hess, x.astype(bf16), preferred_element_type=f32)
            x = (keep * x - linear) - step_size * curve - crew_scr[16 * k + s, :, cols] * c
            used_scr[16 * (k - 1) + s, :, cols] = folded(c * x)
        curve = jnp.dot(hess, x.astype(bf16), preferred_element_type=f32)
        x = (keep * x - linear) - step_size * curve
        used_scr[32 + s, :, cols] = folded(c * x)
        next_ref[0, :, cols] = x

    @pl.when(s == count - 1)
    def _():
        usage_ref[...] = exact_dot(jnp.sum(used_scr[...], axis=1), veh_to_row[...])


def last_kernel(
    slots,
    factors,
    partial_ref,
    linear_ref,
    hess_ref,
    coef_t_ref,
    use_a,
    use_b,
    norms_ref,
    limit_ref,
    dual_ref,
    row_to_veh,
    plan_ref,
    roster_ref,
    sum_a,
    sum_b,
    spread_ref,
    new_dual_ref,
    crew_scr,
):
    s = pl.program_id(0)
    rows = sum_a.shape[1]

    @pl.when(s == 0)
    def _():
        one, two, three = crew_update(
            use_a[0:48] + use_b[0:48], norms_ref[0:1], limit_ref[...], dual_ref[...]
        )
        new_dual_ref[...] = three
        crew_scr[:, 0, :] = step_size * exact_dot(
            jnp.concatenate([one, two], axis=0), row_to_veh[...]
        )
        sum_a[...] = jnp.zeros_like(sum_a)
        sum_b[...] = jnp.zeros_like(sum_b)
        spread_ref[...] = jnp.zeros_like(spread_ref)

    hess = hess_ref[0]
    for cols in lane_chunks(crew_scr.shape[2]):
        c = coef_t_ref[:, cols]
        x = partial_ref[0, :, cols] - crew_scr[s, :, cols] * c
        curve = jnp.dot(hess, x.astype(bf16), preferred_element_type=f32)
        x = (
            (keep * x - linear_ref[0, :, cols])
            - step_size * curve
            - crew_scr[16 + s, :, cols] * c
        )
        turned = x.T
        roster_ref[0, cols, :] = turned
        plan_ref[0, cols, :] = turned.astype(bf16)

    weight, merge, inverse = factors[0, s], factors[1, s], factors[2, s]
    for side, sums in enumerate((sum_a, sum_b)):
        slot = slots[side, s]
        part = 112
        for start in range(0, rows, part):
            x = roster_ref[0, side * rows + start : side * rows + start + part, :]
            held = sums[slot, start : start + part, :]
            gap = held * inverse - x
            squares = gap * gap * merge
            spread_ref[...] += jnp.sum(squares.reshape(part // 8, 8, 128), axis=0)
            sums[slot, start : start + part, :] = held + weight * x


def price_kernel(slots, roster_ref, price_ref, mean_a, mean_b, out_ref):
    s = pl.program_id(0)
    rows = mean_a.shape[1]
    for side, means in enumerate((mean_a, mean_b)):
        slot = slots[side, s]
        part = 112
        for start in range(0, rows, part):
            here = slice(side * rows + start, side * rows + start + part)
            deviation = roster_ref[0, here, :] - means[slot, start : start + part, :]
            out_ref[0, here, :] = (
                price_ref[0, here, :].astype(f32) + penalty * deviation
            ).astype(bf16)


def veh_pairs(kind):
    if kind == "core":
        return [(i, i ^ 1) for i in range(8)]
    return [(z * 2 + c, kind[z] * 2 + c) for z in range(4) for c in range(2)]


def scen_pairs(pair, axis):
    out = []
    for y in range(4):
        for x in range(4):
            to = (y * 4 + pair[x]) if axis == "x" else (pair[y] * 4 + x)
            out.append((y * 4 + x, to))
    return out


def usage_exchange(value):
    value = value + lax.ppermute(value, "veh", veh_pairs("core"))
    value = value + lax.ppermute(value, "veh", veh_pairs(PAIR_A))
    return value, lax.ppermute(value, "veh", veh_pairs(PAIR_B))


def sum_everywhere(value):
    a, b = usage_exchange(value)
    value = a + b
    for axis in ("x", "y"):
        for pair in (PAIR_A, PAIR_B):
            value = value + lax.ppermute(value, "scen", scen_pairs(pair, axis))
    return value


def shift(value, axis, by):
    pairs = []
    for y in range(4):
        for x in range(4):
            to = (y * 4 + (x + by) % 4) if axis == "x" else (((y + by) % 4) * 4 + x)
            pairs.append((y * 4 + x, to))
    return lax.ppermute(value, "scen", pairs)


def merged(parts):
    total, weight = parts[0]
    spread = jnp.zeros((8, 128), f32)
    for other, other_weight in parts[1:]:
        both = weight + other_weight
        factor = jnp.where(both > 0, weight * other_weight / jnp.maximum(both, 1.0), 0.0)
        gap = total / jnp.maximum(weight, 1.0) - other / jnp.maximum(other_weight, 1.0)
        spread = spread + jnp.sum((gap * gap * factor).reshape(-1, 8, 128), axis=0)
        total, weight = total + other, both
    return total, weight, spread


def reduce_half(sums, weight, first, second):
    def w(ef, df):
        return weight(ef, 0)[df][:, None, None]

    up = shift(sums[2][:, 0], first, 1)
    down = shift(sums[2][:, 1], first, -1)
    up, _, s1 = merged([(sums[1][:, 0], w(0, 1)), (up, w(3, 1))])
    down, _, s2 = merged([(sums[3][:, 1], w(0, 3)), (down, w(1, 3))])
    up = shift(jnp.stack([up, sums[1][:, 1]], axis=1), first, 1)
    down = shift(jnp.stack([sums[3][:, 0], down], axis=1), first, -1)
    w0, w1, w2, w3 = (w(e, 0) for e in range(4))
    mine, mine_w, s3 = merged(
        [
            (sums[0], w0[:, None]),
            (up, jnp.stack([w3 + w2, w3], axis=1)),
            (down, jnp.stack([w1, w1 + w2], axis=1)),
        ]
    )
    arrived = [(mine[0], mine_w[0])]
    for by in (1, 3, 2):
        from_row = sum(weight(e, (4 - by) % 4)[0, 0] for e in range(4))
        arrived.append((shift(mine[by], second, by), from_row))
    own, _, s4 = merged(arrived)
    return own, s1 + s2 + s3 + s4


def gather_half(own, first, second):
    row = {0: own}
    for by in (1, 3, 2):
        row[by] = shift(own, second, -by)
    row = jnp.stack([row[k] for k in range(4)], axis=1)
    third = shift(row, first, 1)
    one = shift(row, first, -1)
    two_a = shift(third[0], first, 1)
    two_b = shift(one[1], first, -1)
    two = jnp.stack([two_a, two_b], axis=0)
    return jnp.stack([row, one, two, third], axis=0).transpose(0, 2, 1, 3, 4)


def shards(
    start_plan,
    linear_cost,
    price,
    anchor,
    hessian,
    usage_coef,
    crew_limit,
    crew_dual,
    crew_row,
    bundle_of,
    scen_weight,
):
    count, vehicles, n = start_plan.shape
    crews = crew_limit.shape[1]
    bundle_count = anchor.shape[0]
    me = lax.axis_index("scen")
    my_y, my_x = me // 4, me % 4
    all_bundles = bundle_of[:, 0]
    my_bundles = lax.dynamic_slice_in_dim(all_bundles, me * count, count)
    all_weights = scen_weight.astype(f32)
    my_weights = lax.dynamic_slice_in_dim(all_weights, me * count, count)

    pad = ((0, 0), (0, CREW_PAD - crews))
    limit = jnp.pad(crew_limit, pad)
    dual = jnp.pad(crew_dual, pad)
    crew_ids = jnp.arange(CREW_PAD, dtype=jnp.int32)
    row_to_veh = (crew_ids[:, None] == crew_row[None, :]).astype(bf16)
    veh_to_row = (crew_row[:, None] == crew_ids[None, :]).astype(bf16)

    def per_scen(*shape):
        return pl.BlockSpec((1, *shape), lambda s, *_: (s, 0, 0))

    def whole(*shape):
        return pl.BlockSpec(shape, lambda s, *_: (0,) * len(shape))

    params = pltpu.CompilerParams(
        dimension_semantics=("arbitrary",), vmem_limit_bytes=LIMIT
    )
    tall = jax.ShapeDtypeStruct((count, n, vehicles), f32)
    flat_block = per_scen(vehicles, n)
    tall_block = per_scen(n, vehicles)

    partial, linear, coef_t, usage = pl.pallas_call(
        first_kernel,
        grid_spec=pltpu.PrefetchScalarGridSpec(
            num_scalar_prefetch=1,
            grid=(count,),
            in_specs=[
                flat_block,
                flat_block,
                flat_block,
                pl.BlockSpec((1, vehicles, n), lambda s, b: (b[s], 0, 0)),
                per_scen(n, n),
                whole(vehicles, n),
                whole(count, CREW_PAD),
                whole(CREW_PAD, vehicles),
                whole(vehicles, CREW_PAD),
            ],
            out_specs=[tall_block, tall_block, whole(n, vehicles), whole(56, CREW_PAD)],
            scratch_shapes=[pltpu.VMEM((16, 1, vehicles), f32), pltpu.VMEM((56, 8, vehicles), f32)],
        ),
        out_shape=[
            tall,
            tall,
            jax.ShapeDtypeStruct((n, vehicles), f32),
            jax.ShapeDtypeStruct((56, CREW_PAD), f32),
        ],
        compiler_params=params,
        name="first_steps",
    )(
        my_bundles,
        start_plan,
        linear_cost,
        price,
        anchor,
        hessian,
        usage_coef,
        dual,
        row_to_veh,
        veh_to_row,
    )

    use_a, use_b = usage_exchange(usage)
    norms = use_a[48:56] + use_b[48:56]
    crew_specs = [whole(8, CREW_PAD), whole(count, CREW_PAD), whole(count, CREW_PAD)]
    for _ in range(3):
        partial, usage, dual = pl.pallas_call(
            middle_kernel,
            grid=(count,),
            in_specs=[
                tall_block,
                tall_block,
                per_scen(n, n),
                whole(n, vehicles),
                whole(*use_a.shape),
                whole(*use_a.shape),
                *crew_specs,
                whole(CREW_PAD, vehicles),
                whole(vehicles, CREW_PAD),
            ],
            out_specs=[tall_block, whole(48, CREW_PAD), whole(count, CREW_PAD)],
            out_shape=[
                tall,
                jax.ShapeDtypeStruct((48, CREW_PAD), f32),
                jax.ShapeDtypeStruct((count, CREW_PAD), f32),
            ],
            scratch_shapes=[pltpu.VMEM((48, 1, vehicles), f32), pltpu.VMEM((48, 8, vehicles), f32)],
            compiler_params=params,
            name="three_steps",
        )(partial, linear, hessian, coef_t, use_a, use_b, norms, limit, dual, row_to_veh, veh_to_row)
        use_a, use_b = usage_exchange(usage)

    rel_y = (my_bundles // 4 - my_y + 4) % 4
    rel_x = (my_bundles % 4 - my_x + 4) % 4
    slots = jnp.stack([rel_x * 4 + rel_y, rel_y * 4 + rel_x])
    same = my_bundles[:, None] == my_bundles[None, :]
    before = jnp.arange(count)[None, :] < jnp.arange(count)[:, None]
    held = jnp.sum(jnp.where(same & before, my_weights[None, :], 0.0), axis=1)
    factors = jnp.stack(
        [
            my_weights,
            held * my_weights / (held + my_weights),
            1.0 / jnp.maximum(held, 1.0),
        ]
    )
    half = vehicles // 2
    bundle_sums = jax.ShapeDtypeStruct((bundle_count, half, n), f32)
    plan, roster, sum_a, sum_b, spread, dual = pl.pallas_call(
        last_kernel,
        grid_spec=pltpu.PrefetchScalarGridSpec(
            num_scalar_prefetch=2,
            grid=(count,),
            in_specs=[
                tall_block,
                tall_block,
                per_scen(n, n),
                whole(n, vehicles),
                whole(*use_a.shape),
                whole(*use_a.shape),
                *crew_specs,
                whole(CREW_PAD, vehicles),
            ],
            out_specs=[
                flat_block,
                flat_block,
                whole(bundle_count, half, n),
                whole(bundle_count, half, n),
                whole(8, n),
                whole(count, CREW_PAD),
            ],
            scratch_shapes=[pltpu.VMEM((32, 1, vehicles), f32)],
        ),
        out_shape=[
            jax.ShapeDtypeStruct((count, vehicles, n), bf16),
            jax.ShapeDtypeStruct((count, vehicles, n), f32),
            bundle_sums,
            bundle_sums,
            jax.ShapeDtypeStruct((8, n), f32),
            jax.ShapeDtypeStruct((count, CREW_PAD), f32),
        ],
        compiler_params=params,
        name="last_step",
    )(slots, factors, partial, linear, hessian, coef_t, use_a, use_b, norms, limit, dual, row_to_veh)

    places = jnp.arange(16, dtype=jnp.int32)
    absolute = ((my_y + places // 4) % 4) * 4 + (my_x + places % 4) % 4
    owners = jnp.arange(all_bundles.shape[0], dtype=jnp.int32) // count
    rel_weights = jnp.sum(
        jnp.where(
            (owners[None, None, :] == absolute[:, None, None])
            & (all_bundles[None, None, :] == absolute[None, :, None]),
            all_weights[None, None, :],
            0.0,
        ),
        axis=2,
    ).reshape(4, 4, 4, 4)
    own_weight = jnp.sum(rel_weights[:, :, 0, 0])

    shape5 = (4, 4, 2, half // 2, n)
    own_a, spread_a = reduce_half(
        sum_a.reshape(shape5), lambda ex, ey: rel_weights[ey, ex].T, "x", "y"
    )
    own_b, spread_b = reduce_half(
        sum_b.reshape(shape5), lambda ey, ex: rel_weights[ey, ex], "y", "x"
    )
    own_a, own_b = own_a / own_weight, own_b / own_weight
    mean_a = gather_half(own_a, "x", "y").reshape(bundle_count, half, n)
    mean_b = gather_half(own_b, "y", "x").reshape(bundle_count, half, n)
    spread_total = jnp.sum(sum_everywhere(spread + spread_a + spread_b))
    entries = vehicles * lax.axis_size("veh") * n
    gap = jnp.sqrt(spread_total / (jnp.sum(all_weights) * entries))

    new_price = pl.pallas_call(
        price_kernel,
        grid_spec=pltpu.PrefetchScalarGridSpec(
            num_scalar_prefetch=1,
            grid=(count,),
            in_specs=[
                flat_block,
                flat_block,
                whole(bundle_count, half, n),
                whole(bundle_count, half, n),
            ],
            out_specs=[flat_block],
        ),
        out_shape=[jax.ShapeDtypeStruct((count, vehicles, n), bf16)],
        compiler_params=params,
        name="new_price",
    )(slots, roster, price, mean_a, mean_b)[0]

    own_mean = jnp.concatenate([own_a.reshape(half, n), own_b.reshape(half, n)], axis=0)
    return (plan, new_price, own_mean.astype(bf16)[None], dual[:, :crews], gap)


def solution(mesh):
    return jax.shard_map(
        shards,
        mesh=mesh,
        in_specs=(
            P("scen", "veh", None),
            P("scen", "veh", None),
            P("scen", "veh", None),
            P(None, "veh", None),
            P("scen", None, None),
            P("veh", None),
            P("scen", None),
            P("scen", None),
            P("veh"),
            P(),
            P(),
        ),
        out_specs=(
            P("scen", "veh", None),
            P("scen", "veh", None),
            P("scen", "veh", None),
            P("scen", None),
            P(),
        ),
        check_vma=False,
    )
```

```python
import functools

import jax
import jax.numpy as jnp
import numpy as np
from jax import lax
from jax.experimental import pallas as pl
from jax.experimental.pallas import tpu as pltpu
from jax.sharding import PartitionSpec as P

ITERS = 12
penalty = 1.0
step_size = 0.02
dual_step = 0.02
keep = 1.0 - step_size * penalty
CREW_PAD = 384
LIMIT = 14 * 1024 * 1024
bf16 = jnp.bfloat16
f32 = jnp.float32

PAIR_A = {0: 1, 1: 0, 2: 3, 3: 2}
PAIR_B = {0: 3, 3: 0, 1: 2, 2: 1}


def split3(value):
    hi = value.astype(bf16)
    rest = value - hi.astype(f32)
    mid = rest.astype(bf16)
    low = (rest - mid.astype(f32)).astype(bf16)
    return jnp.concatenate([hi, mid, low], axis=0)


def exact_dot(left, right):
    rows = left.shape[0]
    out = jnp.dot(split3(left), right, preferred_element_type=f32)
    return out[:rows] + out[rows : 2 * rows] + out[2 * rows :]


def folded(value):
    return jnp.sum(value.reshape(-1, 8, value.shape[1]), axis=0)


def used_dot(used, row_to_veh):
    flat = jnp.sum(used, axis=1)
    rows = flat.shape[0]
    out = lax.dot_general(
        split3(flat), row_to_veh, (((1,), (1,)), ((), ())), preferred_element_type=f32
    )
    return out[:rows] + out[rows : 2 * rows] + out[2 * rows :]


def first_kernel(
    bundles,
    start_ref,
    cost_ref,
    price_ref,
    anchor_0,
    anchor_1,
    hess_ref,
    coef_ref,
    dual_ref,
    row_ref,
    partial_ref,
    linear_ref,
    coef_t_ref,
    row_to_veh,
    usage_ref,
    crew_scr,
    used_scr,
    block_scr,
):
    step = pl.program_id(0)
    count = pl.num_programs(0)
    n = hess_ref.shape[-1]

    @pl.when(step == 0)
    def _():
        block_scr[...] = jnp.zeros_like(block_scr)
        ids = lax.broadcasted_iota(jnp.int32, row_to_veh.shape, 0)
        row_to_veh[...] = (ids == row_ref[...]).astype(f32).astype(bf16)
        crew_scr[:, 0, :] = step_size * exact_dot(dual_ref[...], row_to_veh[...])
        used_scr[48:56] = jnp.zeros_like(used_scr[48:56])
        c = coef_ref[...].astype(f32).T
        coef_t_ref[...] = c
        used_scr[48] = folded(c * c)

    block_scr[0:n, 0:n] = hess_ref[0]
    block_scr[n:, n:] = hess_ref[1]
    both = block_scr[...]
    c = coef_t_ref[...]
    s = 2 * step
    xs = []
    for i, anchor_ref in enumerate((anchor_0, anchor_1)):
        linear = step_size * (
            cost_ref[i].astype(f32) + price_ref[i].astype(f32) - penalty * anchor_ref[0].astype(f32)
        )
        linear_ref[s + i] = linear.T
        x = start_ref[i].astype(f32).T
        used_scr[s + i] = folded(c * x)
        xs.append(x)
    for k in (1, 2):
        stacked = jnp.concatenate([x.astype(bf16) for x in xs], axis=0)
        curve = jnp.dot(both, stacked, preferred_element_type=f32)
        for i in range(2):
            x = (keep * xs[i] - linear_ref[s + i]) - step_size * curve[i * n : (i + 1) * n]
            if k < 2:
                x = x - crew_scr[s + i] * c
            used_scr[16 * k + s + i] = folded(c * x)
            xs[i] = x
    for i in range(2):
        partial_ref[s + i] = xs[i]

    @pl.when(step == count - 1)
    def _():
        usage_ref[...] = used_dot(used_scr[...], row_to_veh[...])


def crew_update(usage, norms, limit, dual):
    one = jnp.maximum(dual + dual_step * (usage[0:16] - limit), 0.0)
    third = usage[32:48] - step_size * one * norms
    two = jnp.maximum(one + dual_step * (usage[16:32] - limit), 0.0)
    three = jnp.maximum(two + dual_step * (third - limit), 0.0)
    return one, two, three


def middle_kernel(
    partial_ref,
    linear_ref,
    hess_ref,
    coef_t_ref,
    use_a,
    use_b,
    norms_ref,
    limit_ref,
    dual_ref,
    row_to_veh,
    next_ref,
    usage_ref,
    new_dual_ref,
    crew_scr,
    used_scr,
    block_scr,
):
    count = partial_ref.shape[0]
    n = hess_ref.shape[-1]
    one, two, three = crew_update(
        use_a[0:48] + use_b[0:48], norms_ref[0:1], limit_ref[...], dual_ref[...]
    )
    new_dual_ref[...] = three
    crew_scr[:, 0, :] = step_size * exact_dot(
        jnp.concatenate([one, two, three], axis=0), row_to_veh[...]
    )
    block_scr[...] = jnp.zeros_like(block_scr)

    def two_scenarios(pair, carry):
        s = 2 * pair
        block_scr[0:n, 0:n] = hess_ref[s]
        block_scr[n:, n:] = hess_ref[s + 1]
        both = block_scr[...]
        c = coef_t_ref[...]
        xs = [partial_ref[s + i] - crew_scr[s + i] * c for i in range(2)]
        for k in (1, 2, 3):
            stacked = jnp.concatenate([x.astype(bf16) for x in xs], axis=0)
            curve = jnp.dot(both, stacked, preferred_element_type=f32)
            for i in range(2):
                x = (keep * xs[i] - linear_ref[s + i]) - step_size * curve[i * n : (i + 1) * n]
                if k < 3:
                    x = x - crew_scr[16 * k + s + i] * c
                used_scr[16 * (k - 1) + s + i] = folded(c * x)
                xs[i] = x
        for i in range(2):
            next_ref[s + i] = xs[i]
        return carry

    lax.fori_loop(0, count // 2, two_scenarios, 0)
    usage_ref[...] = used_dot(used_scr[...], row_to_veh[...])


def last_kernel(
    slots,
    factors,
    partial_ref,
    linear_ref,
    hess_ref,
    coef_t_ref,
    use_a,
    use_b,
    norms_ref,
    limit_ref,
    dual_ref,
    row_to_veh,
    plan_ref,
    roster_ref,
    sum_a,
    sum_b,
    send_au,
    send_ad,
    send_bu,
    send_bd,
    spread_ref,
    new_dual_ref,
    crew_scr,
):
    s = pl.program_id(0)
    count = pl.num_programs(0)
    rows = sum_a.shape[1]

    @pl.when(s == 0)
    def _():
        one, two, three = crew_update(
            use_a[0:48] + use_b[0:48], norms_ref[0:1], limit_ref[...], dual_ref[...]
        )
        new_dual_ref[...] = three
        crew_scr[:, 0, :] = step_size * exact_dot(
            jnp.concatenate([one, two], axis=0), row_to_veh[...]
        )
        sum_a[...] = jnp.zeros_like(sum_a)
        sum_b[...] = jnp.zeros_like(sum_b)
        spread_ref[...] = jnp.zeros_like(spread_ref)

    c = coef_t_ref[...]
    x = partial_ref[s] - crew_scr[s] * c
    curve = jnp.dot(hess_ref[s], x.astype(bf16), preferred_element_type=f32)
    x = (keep * x - linear_ref[s]) - step_size * curve - crew_scr[16 + s] * c
    roster_ref[s] = x.T

    weight, merge, inverse = factors[0, s], factors[1, s], factors[2, s]
    part = 112
    spread = jnp.zeros((8, 128), f32)
    for side, sums in enumerate((sum_a, sum_b)):
        slot = slots[side, s]
        for start in range(0, rows, part):
            here = pl.ds(side * rows + start, part)
            x = roster_ref[s, here, :]
            plan_ref[0, here, :] = x.astype(bf16)
            held = sums[slot, start : start + part, :]
            gap = held * inverse - x
            spread = spread + merge * folded(gap * gap)
            sums[slot, start : start + part, :] = held + weight * x
    spread_ref[...] += spread

    @pl.when(s == count - 1)
    def _():
        for sums, up, down in ((sum_a, send_au, send_ad), (sum_b, send_bu, send_bd)):
            for k in range(4):
                up[k] = sums[8 + k, : rows // 2, :]
                down[k] = sums[8 + k, rows // 2 :, :]


def merge_into(total, weight, other, other_weight):
    weight = jnp.full((8, 128), weight, f32)
    other_weight = jnp.full((8, 128), other_weight, f32)
    both = weight + other_weight
    factor = jnp.where(both > 0, weight * other_weight / jnp.maximum(both, 1.0), 0.0)
    shape = total.shape
    total8, other8 = total.reshape(-1, 8, 128), other.reshape(-1, 8, 128)
    gap = total8 * (1.0 / jnp.maximum(weight, 1.0)) - other8 * (1.0 / jnp.maximum(other_weight, 1.0))
    return total + other, factor * jnp.sum(gap * gap, axis=0)


def forward_kernel(weights, sums, up_in, down_in, up_out, down_out, spread_ref):
    rows = sums.shape[1] // 2
    spread = jnp.zeros((8, 128), f32)
    for k in range(4):
        total, more = merge_into(sums[4 + k, :rows, :], weights[0, 4 + k], up_in[k], weights[12, 4 + k])
        spread += more
        up_out[0, k] = total
        up_out[1, k] = sums[4 + k, rows:, :]
        down_out[0, k] = sums[12 + k, :rows, :]
        total, more = merge_into(
            sums[12 + k, rows:, :], weights[0, 12 + k], down_in[k], weights[4, 12 + k]
        )
        spread += more
        down_out[1, k] = total
    spread_ref[...] = spread


def arrive_kernel(weights, sums, up_in, down_in, own, out_1, out_2, out_3, spread_ref):
    rows = sums.shape[1] // 2
    spread = jnp.zeros((8, 128), f32)
    for k, out in enumerate((own, out_1, out_2, out_3)):
        w0, w1, w2, w3 = (weights[4 * e, k] for e in range(4))
        for half in range(2):
            here = slice(half * rows, (half + 1) * rows)
            w_up, w_down = (w3 + w2, w1) if half == 0 else (w3, w1 + w2)
            total, more = merge_into(sums[k, here, :], w0, up_in[half, k], w_up)
            spread += more
            total, more = merge_into(total, w0 + w_up, down_in[half, k], w_down)
            spread += more
            out[here, :] = total
    spread_ref[...] = spread


def finish_kernel(weights, own, in_1, in_2, in_3, mean_ref, spread_ref):
    line = [sum(weights[4 * e + j, 0] for e in range(4)) for j in range(4)]
    total, weight = own[...], line[0]
    spread = jnp.zeros((8, 128), f32)
    for by, part in ((1, in_1), (3, in_3), (2, in_2)):
        total, more = merge_into(total, weight, part[...], line[4 - by])
        spread += more
        weight = weight + line[4 - by]
    mean_ref[...] = total / jnp.full((8, 128), weight, f32)[0:1]
    spread_ref[...] = spread


def price_kernel(slots, roster_ref, price_ref, spread_ref, weight_ref, *refs):
    means, out_ref, gap_ref = refs[:10], refs[10], refs[11]
    each = price_ref.shape[0]
    rows = means[3].shape[1]

    @pl.when(pl.program_id(0) == 0)
    def _():
        spread = jnp.sum(spread_ref[...], keepdims=True)
        gap_ref[...] = jnp.sqrt(spread / jnp.sum(weight_ref[...], keepdims=True))

    for i in range(each):
        s = pl.program_id(0) * each + i
        for side in range(2):
            slot = slots[side, s]
            first, second = slot // 4, slot % 4
            pack, one, third, two_low, two_high = means[side * 5 : side * 5 + 5]
            for k in range(4):

                @pl.when(first == k)
                def _():
                    for half in range(2):
                        if k == 2:
                            mean = (two_low, two_high)[half][second]
                        else:
                            mean = (pack, one, None, third)[k][half, second]
                        here = pl.ds((side * 2 + half) * rows, rows)
                        deviation = roster_ref[s, here, :] - mean
                        out_ref[i, here, :] = (
                            price_ref[i, here, :].astype(f32) + penalty * deviation
                        ).astype(bf16)


def veh_pairs(kind):
    if kind == "core":
        return [(i, i ^ 1) for i in range(8)]
    return [(z * 2 + c, kind[z] * 2 + c) for z in range(4) for c in range(2)]


def scen_pairs(pair, axis):
    out = []
    for y in range(4):
        for x in range(4):
            to = (y * 4 + pair[x]) if axis == "x" else (pair[y] * 4 + x)
            out.append((y * 4 + x, to))
    return out


def usage_exchange(value):
    value = value + lax.ppermute(value, "veh", veh_pairs("core"))
    value = value + lax.ppermute(value, "veh", veh_pairs(PAIR_A))
    return value, lax.ppermute(value, "veh", veh_pairs(PAIR_B))


def sum_everywhere(value):
    a, b = usage_exchange(value)
    value = a + b
    for axis in ("x", "y"):
        for pair in (PAIR_A, PAIR_B):
            value = value + lax.ppermute(value, "scen", scen_pairs(pair, axis))
    return value


def shift(value, axis, by):
    pairs = []
    for y in range(4):
        for x in range(4):
            to = (y * 4 + (x + by) % 4) if axis == "x" else (((y + by) % 4) * 4 + x)
            pairs.append((y * 4 + x, to))
    return lax.ppermute(value, "scen", pairs)


def vmem_spec():
    return pl.BlockSpec(memory_space=pltpu.VMEM)


def in_vmem(value):
    return pltpu.with_memory_space_constraint(value, pltpu.VMEM)


def in_hbm(value):
    return pltpu.with_memory_space_constraint(value, pltpu.HBM)


def local_call(body, weights, arrays, out_shapes, name):
    return pl.pallas_call(
        body,
        in_specs=[pl.BlockSpec(memory_space=pltpu.SMEM)] + [vmem_spec()] * len(arrays),
        out_specs=[vmem_spec()] * (len(out_shapes) + 1),
        out_shape=[pltpu.VMEM(shape, f32) for shape in out_shapes] + [pltpu.VMEM((8, 128), f32)],
        compiler_params=pltpu.CompilerParams(vmem_limit_bytes=LIMIT),
        name=name,
    )(weights, *[in_vmem(a) for a in arrays])


def gather_row(own, second):
    return {0: own, **{by: shift(own, second, -by) for by in (1, 3, 2)}}


def gather_half(row, first):
    rows = row[0].shape[0] // 2
    pack = jnp.stack([row[k].reshape(2, rows, -1) for k in range(4)], axis=1)
    third = shift(pack, first, 1)
    one = shift(pack, first, -1)
    two_low = shift(third[0], first, 1)
    two_high = shift(one[1], first, -1)
    return [pack, one, third, two_low, two_high]


def shards(
    start_plan,
    linear_cost,
    price,
    anchor,
    hessian,
    usage_coef,
    crew_limit,
    crew_dual,
    crew_row,
    bundle_of,
    scen_weight,
):
    count, vehicles, n = start_plan.shape
    crews = crew_limit.shape[1]
    bundle_count = anchor.shape[0]
    me = lax.axis_index("scen")
    all_bundles = bundle_of[:, 0]
    my_bundles = lax.dynamic_slice_in_dim(all_bundles, me * count, count)
    all_weights = scen_weight.astype(f32)
    my_weights = lax.dynamic_slice_in_dim(all_weights, me * count, count)

    pad = ((0, 0), (0, CREW_PAD - crews))
    limit = jnp.pad(crew_limit, pad)
    dual = jnp.pad(crew_dual, pad)
    def per_scen(*shape):
        return pl.BlockSpec((1, *shape), lambda s, *_: (s, 0, 0))

    def whole(*shape):
        return pl.BlockSpec(shape, lambda s, *_: (0,) * len(shape))

    params = pltpu.CompilerParams(
        dimension_semantics=("arbitrary",), vmem_limit_bytes=LIMIT
    )
    tall = pltpu.VMEM((count, n, vehicles), f32)
    flat_block = per_scen(vehicles, n)
    pair_block = pl.BlockSpec((2, vehicles, n), lambda s, *_: (s, 0, 0))
    vm = vmem_spec()

    partial, linear, coef_t, row_to_veh, usage = pl.pallas_call(
        first_kernel,
        grid_spec=pltpu.PrefetchScalarGridSpec(
            num_scalar_prefetch=1,
            grid=(count // 2,),
            in_specs=[
                pair_block,
                pair_block,
                pair_block,
                pl.BlockSpec((1, vehicles, n), lambda s, b: (b[2 * s], 0, 0)),
                pl.BlockSpec((1, vehicles, n), lambda s, b: (b[2 * s + 1], 0, 0)),
                pl.BlockSpec((2, n, n), lambda s, *_: (s, 0, 0)),
                whole(vehicles, n),
                whole(count, CREW_PAD),
                whole(1, vehicles),
            ],
            out_specs=[vm] * 5,
            scratch_shapes=[
                pltpu.VMEM((16, 1, vehicles), f32),
                pltpu.VMEM((56, 8, vehicles), f32),
                pltpu.VMEM((2 * n, 2 * n), bf16),
            ],
        ),
        out_shape=[
            tall,
            tall,
            pltpu.VMEM((n, vehicles), f32),
            pltpu.VMEM((CREW_PAD, vehicles), bf16),
            pltpu.VMEM((56, CREW_PAD), f32),
        ],
        compiler_params=params,
        name="first_steps",
    )(
        my_bundles,
        in_hbm(start_plan),
        in_hbm(linear_cost),
        in_hbm(price),
        in_hbm(anchor),
        in_hbm(anchor),
        hessian,
        usage_coef,
        dual,
        crew_row[None, :],
    )

    use_a, use_b = usage_exchange(usage)
    norms = use_a[48:56] + use_b[48:56]
    for _ in range(3):
        partial, usage, dual = pl.pallas_call(
            middle_kernel,
            in_specs=[vm] * 10,
            out_specs=[vm] * 3,
            out_shape=[
                tall,
                pltpu.VMEM((48, CREW_PAD), f32),
                pltpu.VMEM((count, CREW_PAD), f32),
            ],
            input_output_aliases={0: 0},
            scratch_shapes=[
                pltpu.VMEM((48, 1, vehicles), f32),
                pltpu.VMEM((48, 8, vehicles), f32),
                pltpu.VMEM((2 * n, 2 * n), bf16),
            ],
            compiler_params=pltpu.CompilerParams(vmem_limit_bytes=LIMIT),
            name="three_steps",
        )(
            *[
                in_vmem(a)
                for a in (
                    partial,
                    linear,
                    hessian,
                    coef_t,
                    use_a,
                    use_b,
                    norms,
                    limit,
                    dual,
                    row_to_veh,
                )
            ]
        )
        use_a, use_b = usage_exchange(usage)

    me_y, me_x = np.arange(16)[:, None] // 4, np.arange(16)[:, None] % 4
    it_y, it_x = np.arange(16)[None, :] // 4, np.arange(16)[None, :] % 4
    place_a = ((it_x - me_x) % 4) * 4 + (it_y - me_y) % 4
    place_b = ((it_y - me_y) % 4) * 4 + (it_x - me_x) % 4
    here = jnp.arange(16, dtype=jnp.int32) == me
    row_a = jnp.sum(jnp.where(here[:, None], place_a, 0), axis=0)
    row_b = jnp.sum(jnp.where(here[:, None], place_b, 0), axis=0)
    ids = jnp.arange(16, dtype=jnp.int32)
    hot = my_bundles[:, None] == ids[None, :]
    slots = jnp.stack(
        [jnp.sum(jnp.where(hot, row[None, :], 0), axis=1) for row in (row_a, row_b)]
    ).astype(jnp.int32)
    same = my_bundles[:, None] == my_bundles[None, :]
    before = jnp.arange(count)[None, :] < jnp.arange(count)[:, None]
    held = jnp.sum(jnp.where(same & before, my_weights[None, :], 0.0), axis=1)
    factors = jnp.stack(
        [
            my_weights,
            held * my_weights / (held + my_weights),
            1.0 / jnp.maximum(held, 1.0),
        ]
    )
    half = vehicles // 2
    bundle_sums = pltpu.VMEM((bundle_count, half, n), f32)
    quarter = pltpu.VMEM((4, half // 2, n), f32)
    plan, roster, sum_a, sum_b, up_a, down_a, up_b, down_b, spread, dual = pl.pallas_call(
        last_kernel,
        grid_spec=pltpu.PrefetchScalarGridSpec(
            num_scalar_prefetch=2,
            grid=(count,),
            in_specs=[vm] * 10,
            out_specs=[flat_block] + [vm] * 9,
            scratch_shapes=[pltpu.VMEM((32, 1, vehicles), f32)],
        ),
        out_shape=[
            jax.ShapeDtypeStruct((count, vehicles, n), bf16),
            pltpu.VMEM((count, vehicles, n), f32),
            bundle_sums,
            bundle_sums,
            quarter,
            quarter,
            quarter,
            quarter,
            pltpu.VMEM((8, n), f32),
            pltpu.VMEM((count, CREW_PAD), f32),
        ],
        compiler_params=params,
        name="last_step",
    )(
        slots,
        factors,
        *[
            in_vmem(a)
            for a in (
                partial,
                linear,
                hessian,
                coef_t,
                use_a,
                use_b,
                norms,
                limit,
                dual,
                row_to_veh,
            )
        ],
    )

    owners = jnp.arange(all_bundles.shape[0], dtype=jnp.int32) // count

    def weight_table(row):
        device = jnp.sum(jnp.where(owners[:, None] == ids[None, :], row[None, :], 0), axis=1)
        bundle = jnp.sum(jnp.where(all_bundles[:, None] == ids[None, :], row[None, :], 0), axis=1)
        return jnp.sum(
            jnp.where(
                (device[None, None, :] == ids[:, None, None])
                & (bundle[None, None, :] == ids[None, :, None]),
                all_weights[None, None, :],
                0.0,
            ),
            axis=2,
        )

    weights_a = weight_table(row_a)
    weights_b = weight_table(row_b)

    sides = (
        ("x", "y", weights_a, sum_a, up_a, down_a),
        ("y", "x", weights_b, sum_b, up_b, down_b),
    )
    flow = (2, 4, half // 2, n)
    flat = (half, n)
    moved = [(shift(up, f, 1), shift(down, f, -1)) for f, _, _, _, up, down in sides]
    moved = [
        local_call(forward_kernel, w, (sums, up, down), [flow, flow], "forward")
        for (_, _, w, sums, _, _), (up, down) in zip(sides, moved)
    ]
    spreads = [spread] + [m[2] for m in moved]
    moved = [(shift(m[0], side[0], 1), shift(m[1], side[0], -1)) for side, m in zip(sides, moved)]
    moved = [
        local_call(arrive_kernel, w, (sums, up, down), [flat] * 4, "arrive")
        for (_, _, w, sums, _, _), (up, down) in zip(sides, moved)
    ]
    spreads += [m[4] for m in moved]
    moved = [
        (m[0], *[shift(m[by], side[1], by) for by in (1, 2, 3)]) for side, m in zip(sides, moved)
    ]
    moved = [
        local_call(finish_kernel, side[2], m, [flat], "finish") for side, m in zip(sides, moved)
    ]
    spreads += [m[1] for m in moved]
    own_a, own_b = moved[0][0], moved[1][0]
    row_a, row_b = gather_row(own_a, "y"), gather_row(own_b, "x")
    row_a, row_b, spread = lax.optimization_barrier((row_a, row_b, sum(spreads)))
    means = gather_half(row_a, "x") + gather_half(row_b, "y")
    spread_total = sum_everywhere(spread)
    entries = vehicles * lax.axis_size("veh") * n

    each = 2
    new_price, gap = pl.pallas_call(
        price_kernel,
        grid_spec=pltpu.PrefetchScalarGridSpec(
            num_scalar_prefetch=1,
            grid=(count // each,),
            in_specs=[vm, pair_block] + [vm] * 12,
            out_specs=[pair_block, whole(1, 1)],
        ),
        out_shape=[
            jax.ShapeDtypeStruct((count, vehicles, n), bf16),
            jax.ShapeDtypeStruct((1, 1), f32),
        ],
        compiler_params=params,
        name="new_price",
    )(
        slots,
        in_vmem(roster),
        in_hbm(price),
        in_vmem(spread_total),
        in_vmem((all_weights * entries)[None, :]),
        *[in_vmem(m) for m in means],
    )

    own_mean = jnp.concatenate([own_a, own_b], axis=0)
    return (plan, new_price, own_mean.astype(bf16)[None], dual[:, :crews], gap[0, 0])


def solution(mesh):
    return jax.shard_map(
        shards,
        mesh=mesh,
        in_specs=(
            P("scen", "veh", None),
            P("scen", "veh", None),
            P("scen", "veh", None),
            P(None, "veh", None),
            P("scen", None, None),
            P("veh", None),
            P("scen", None),
            P("scen", None),
            P("veh"),
            P(),
            P(),
        ),
        out_specs=(
            P("scen", "veh", None),
            P("scen", "veh", None),
            P("scen", "veh", None),
            P("scen", None),
            P(),
        ),
        check_vma=False,
    )
```

```python
import functools

import jax
import jax.numpy as jnp
import numpy as np
from jax import lax
from jax.experimental import pallas as pl
from jax.experimental.pallas import tpu as pltpu
from jax.sharding import PartitionSpec as P

ITERS = 12
penalty = 1.0
step_size = 0.02
dual_step = 0.02
keep = 1.0 - step_size * penalty
CREW_PAD = 384
LIMIT = 14 * 1024 * 1024
bf16 = jnp.bfloat16
f32 = jnp.float32

PAIR_A = {0: 1, 1: 0, 2: 3, 3: 2}
PAIR_B = {0: 3, 3: 0, 1: 2, 2: 1}


def split3(value):
    hi = value.astype(bf16)
    rest = value - hi.astype(f32)
    mid = rest.astype(bf16)
    low = (rest - mid.astype(f32)).astype(bf16)
    return jnp.concatenate([hi, mid, low], axis=0)


def exact_dot(left, right):
    rows = left.shape[0]
    out = jnp.dot(split3(left), right, preferred_element_type=f32)
    return out[:rows] + out[rows : 2 * rows] + out[2 * rows :]


def folded(value):
    return jnp.sum(value.reshape(-1, 8, value.shape[1]), axis=0)


def used_dot(used, row_to_veh):
    flat = jnp.sum(used, axis=1)
    rows = flat.shape[0]
    out = lax.dot_general(
        split3(flat), row_to_veh, (((1,), (1,)), ((), ())), preferred_element_type=f32
    )
    return out[:rows] + out[rows : 2 * rows] + out[2 * rows :]


def first_kernel(
    bundles,
    start_ref,
    cost_ref,
    price_ref,
    anchor_0,
    anchor_1,
    hess_ref,
    coef_ref,
    dual_ref,
    row_ref,
    partial_ref,
    linear_ref,
    coef_t_ref,
    row_to_veh,
    usage_ref,
    crew_scr,
    used_scr,
    block_scr,
):
    step = pl.program_id(0)
    count = pl.num_programs(0)
    n = hess_ref.shape[-1]

    @pl.when(step == 0)
    def _():
        block_scr[...] = jnp.zeros_like(block_scr)
        ids = lax.broadcasted_iota(jnp.int32, row_to_veh.shape, 0)
        row_to_veh[...] = (ids == row_ref[...]).astype(f32).astype(bf16)
        crew_scr[:, 0, :] = step_size * exact_dot(dual_ref[...], row_to_veh[...])
        used_scr[48:56] = jnp.zeros_like(used_scr[48:56])
        c = coef_ref[...].astype(f32).T
        coef_t_ref[...] = c
        used_scr[48] = folded(c * c)

    block_scr[0:n, 0:n] = hess_ref[0]
    block_scr[n:, n:] = hess_ref[1]
    both = block_scr[...]
    c = coef_t_ref[...]
    s = 2 * step
    xs = []
    for i, anchor_ref in enumerate((anchor_0, anchor_1)):
        linear = step_size * (
            cost_ref[i].astype(f32) + price_ref[i].astype(f32) - penalty * anchor_ref[0].astype(f32)
        )
        linear_ref[s + i] = linear.T
        x = start_ref[i].astype(f32).T
        used_scr[s + i] = folded(c * x)
        xs.append(x)
    for k in (1, 2):
        stacked = jnp.concatenate([x.astype(bf16) for x in xs], axis=0)
        curve = jnp.dot(both, stacked, preferred_element_type=f32)
        for i in range(2):
            x = (keep * xs[i] - linear_ref[s + i]) - step_size * curve[i * n : (i + 1) * n]
            if k < 2:
                x = x - crew_scr[s + i] * c
            used_scr[16 * k + s + i] = folded(c * x)
            xs[i] = x
    for i in range(2):
        partial_ref[s + i] = xs[i]

    @pl.when(step == count - 1)
    def _():
        usage_ref[...] = used_dot(used_scr[...], row_to_veh[...])


def crew_update(usage, norms, limit, dual):
    one = jnp.maximum(dual + dual_step * (usage[0:16] - limit), 0.0)
    third = usage[32:48] - step_size * one * norms
    two = jnp.maximum(one + dual_step * (usage[16:32] - limit), 0.0)
    three = jnp.maximum(two + dual_step * (third - limit), 0.0)
    return one, two, three


def middle_kernel(
    partial_ref,
    linear_ref,
    hess_ref,
    coef_t_ref,
    use_a,
    use_b,
    norms_ref,
    limit_ref,
    dual_ref,
    row_to_veh,
    next_ref,
    usage_ref,
    new_dual_ref,
    crew_scr,
    used_scr,
    block_scr,
):
    count = partial_ref.shape[0]
    n = hess_ref.shape[-1]
    one, two, three = crew_update(
        use_a[0:48] + use_b[0:48], norms_ref[0:1], limit_ref[...], dual_ref[...]
    )
    new_dual_ref[...] = three
    crew_scr[:, 0, :] = step_size * exact_dot(
        jnp.concatenate([one, two, three], axis=0), row_to_veh[...]
    )
    block_scr[...] = jnp.zeros_like(block_scr)

    def two_scenarios(pair, carry):
        s = 2 * pair
        block_scr[0:n, 0:n] = hess_ref[s]
        block_scr[n:, n:] = hess_ref[s + 1]
        both = block_scr[...]
        c = coef_t_ref[...]
        xs = [partial_ref[s + i] - crew_scr[s + i] * c for i in range(2)]
        for k in (1, 2, 3):
            stacked = jnp.concatenate([x.astype(bf16) for x in xs], axis=0)
            curve = jnp.dot(both, stacked, preferred_element_type=f32)
            for i in range(2):
                x = (keep * xs[i] - linear_ref[s + i]) - step_size * curve[i * n : (i + 1) * n]
                if k < 3:
                    x = x - crew_scr[16 * k + s + i] * c
                used_scr[16 * (k - 1) + s + i] = folded(c * x)
                xs[i] = x
        for i in range(2):
            next_ref[s + i] = xs[i]
        return carry

    lax.fori_loop(0, count // 2, two_scenarios, 0)
    usage_ref[...] = used_dot(used_scr[...], row_to_veh[...])


def last_kernel(
    slots,
    factors,
    partial_ref,
    linear_ref,
    hess_ref,
    coef_t_ref,
    use_a,
    use_b,
    norms_ref,
    limit_ref,
    dual_ref,
    row_to_veh,
    plan_ref,
    roster_ref,
    sum_a,
    sum_b,
    send_au,
    send_ad,
    send_bu,
    send_bd,
    spread_ref,
    new_dual_ref,
    crew_scr,
):
    s = pl.program_id(0)
    count = pl.num_programs(0)
    rows = sum_a.shape[1]

    @pl.when(s == 0)
    def _():
        one, two, three = crew_update(
            use_a[0:48] + use_b[0:48], norms_ref[0:1], limit_ref[...], dual_ref[...]
        )
        new_dual_ref[...] = three
        crew_scr[:, 0, :] = step_size * exact_dot(
            jnp.concatenate([one, two], axis=0), row_to_veh[...]
        )
        sum_a[...] = jnp.zeros_like(sum_a)
        sum_b[...] = jnp.zeros_like(sum_b)
        spread_ref[...] = jnp.zeros_like(spread_ref)

    c = coef_t_ref[...]
    x = partial_ref[s] - crew_scr[s] * c
    curve = jnp.dot(hess_ref[s], x.astype(bf16), preferred_element_type=f32)
    x = (keep * x - linear_ref[s]) - step_size * curve - crew_scr[16 + s] * c
    roster_ref[s] = x.T

    weight, merge, inverse = factors[0, s], factors[1, s], factors[2, s]
    part = 112
    spread = jnp.zeros((8, 128), f32)
    for side, sums in enumerate((sum_a, sum_b)):
        slot = slots[side, s]
        for start in range(0, rows, part):
            here = pl.ds(side * rows + start, part)
            x = roster_ref[s, here, :]
            plan_ref[0, here, :] = x.astype(bf16)
            held = sums[slot, start : start + part, :]
            gap = held * inverse - x
            spread = spread + merge * folded(gap * gap)
            sums[slot, start : start + part, :] = held + weight * x
    spread_ref[...] += spread

    @pl.when(s == count - 1)
    def _():
        for sums, up, down in ((sum_a, send_au, send_ad), (sum_b, send_bu, send_bd)):
            for k in range(4):
                up[k] = sums[8 + k, : rows // 2, :]
                down[k] = sums[8 + k, rows // 2 :, :]


def merge_into(total, weight, other, other_weight):
    weight = jnp.full((8, 128), weight, f32)
    other_weight = jnp.full((8, 128), other_weight, f32)
    both = weight + other_weight
    factor = jnp.where(both > 0, weight * other_weight / jnp.maximum(both, 1.0), 0.0)
    shape = total.shape
    total8, other8 = total.reshape(-1, 8, 128), other.reshape(-1, 8, 128)
    gap = total8 * (1.0 / jnp.maximum(weight, 1.0)) - other8 * (1.0 / jnp.maximum(other_weight, 1.0))
    return total + other, factor * jnp.sum(gap * gap, axis=0)


def forward_kernel(weights, sums, up_in, down_in, up_out, down_out, spread_ref):
    rows = sums.shape[1] // 2
    spread = jnp.zeros((8, 128), f32)
    for k in range(4):
        total, more = merge_into(sums[4 + k, :rows, :], weights[0, 4 + k], up_in[k], weights[12, 4 + k])
        spread += more
        up_out[0, k] = total
        up_out[1, k] = sums[4 + k, rows:, :]
        down_out[0, k] = sums[12 + k, :rows, :]
        total, more = merge_into(
            sums[12 + k, rows:, :], weights[0, 12 + k], down_in[k], weights[4, 12 + k]
        )
        spread += more
        down_out[1, k] = total
    spread_ref[...] = spread


def arrive_kernel(weights, sums, up_in, down_in, own, out_1, out_2, out_3, spread_ref):
    rows = sums.shape[1] // 2
    spread = jnp.zeros((8, 128), f32)
    for k, out in enumerate((own, out_1, out_2, out_3)):
        w0, w1, w2, w3 = (weights[4 * e, k] for e in range(4))
        for half in range(2):
            here = slice(half * rows, (half + 1) * rows)
            w_up, w_down = (w3 + w2, w1) if half == 0 else (w3, w1 + w2)
            total, more = merge_into(sums[k, here, :], w0, up_in[half, k], w_up)
            spread += more
            total, more = merge_into(total, w0 + w_up, down_in[half, k], w_down)
            spread += more
            out[here, :] = total
    spread_ref[...] = spread


def finish_kernel(weights, own, in_1, in_2, in_3, mean_ref, spread_ref):
    line = [sum(weights[4 * e + j, 0] for e in range(4)) for j in range(4)]
    total, weight = own[...], line[0]
    spread = jnp.zeros((8, 128), f32)
    for by, part in ((1, in_1), (3, in_3), (2, in_2)):
        total, more = merge_into(total, weight, part[...], line[4 - by])
        spread += more
        weight = weight + line[4 - by]
    mean_ref[...] = total / jnp.full((8, 128), weight, f32)[0:1]
    spread_ref[...] = spread


def price_kernel(slots, roster_ref, price_ref, spread_ref, weight_ref, *refs):
    means, out_ref, gap_ref = refs[:10], refs[10], refs[11]
    each = price_ref.shape[0]
    rows = means[3].shape[1]

    @pl.when(pl.program_id(0) == 0)
    def _():
        spread = jnp.sum(spread_ref[...], keepdims=True)
        gap_ref[...] = jnp.sqrt(spread / jnp.sum(weight_ref[...], keepdims=True))

    for i in range(each):
        s = pl.program_id(0) * each + i
        for side in range(2):
            slot = slots[side, s]
            first, second = slot // 4, slot % 4
            pack, one, third, two_low, two_high = means[side * 5 : side * 5 + 5]
            for k in range(4):

                @pl.when(first == k)
                def _():
                    for half in range(2):
                        if k == 2:
                            mean = (two_low, two_high)[half][second]
                        else:
                            mean = (pack, one, None, third)[k][half, second]
                        here = pl.ds((side * 2 + half) * rows, rows)
                        deviation = roster_ref[s, here, :] - mean
                        out_ref[i, here, :] = (
                            price_ref[i, here, :].astype(f32) + penalty * deviation
                        ).astype(bf16)


def veh_pairs(kind):
    if kind == "core":
        return [(i, i ^ 1) for i in range(8)]
    return [(z * 2 + c, kind[z] * 2 + c) for z in range(4) for c in range(2)]


def scen_pairs(pair, axis):
    out = []
    for y in range(4):
        for x in range(4):
            to = (y * 4 + pair[x]) if axis == "x" else (pair[y] * 4 + x)
            out.append((y * 4 + x, to))
    return out


def usage_exchange(value):
    value = value + lax.ppermute(value, "veh", veh_pairs("core"))
    value = value + lax.ppermute(value, "veh", veh_pairs(PAIR_A))
    return value, lax.ppermute(value, "veh", veh_pairs(PAIR_B))


def sum_over_scen(value):
    for axis in ("x", "y"):
        for pair in (PAIR_A, PAIR_B):
            value = value + lax.ppermute(value, "scen", scen_pairs(pair, axis))
    return value


def shift(value, axis, by):
    pairs = []
    for y in range(4):
        for x in range(4):
            to = (y * 4 + (x + by) % 4) if axis == "x" else (((y + by) % 4) * 4 + x)
            pairs.append((y * 4 + x, to))
    return lax.ppermute(value, "scen", pairs)


def vmem_spec():
    return pl.BlockSpec(memory_space=pltpu.VMEM)


def in_vmem(value):
    return pltpu.with_memory_space_constraint(value, pltpu.VMEM)


def in_hbm(value):
    return pltpu.with_memory_space_constraint(value, pltpu.HBM)


def local_call(body, weights, arrays, out_shapes, name):
    return pl.pallas_call(
        body,
        in_specs=[pl.BlockSpec(memory_space=pltpu.SMEM)] + [vmem_spec()] * len(arrays),
        out_specs=[vmem_spec()] * (len(out_shapes) + 1),
        out_shape=[pltpu.VMEM(shape, f32) for shape in out_shapes] + [pltpu.VMEM((8, 128), f32)],
        compiler_params=pltpu.CompilerParams(vmem_limit_bytes=LIMIT),
        name=name,
    )(weights, *[in_vmem(a) for a in arrays])


def gather_row(own, second):
    return {0: own, **{by: shift(own, second, -by) for by in (1, 3, 2)}}


def gather_near(row, first):
    rows = row[0].shape[0] // 2
    pack = jnp.stack([row[k].reshape(2, rows, -1) for k in range(4)], axis=1)
    return pack, shift(pack, first, -1), shift(pack, first, 1)


def gather_far(pack, one, third, first):
    two_low = shift(third[0], first, 1)
    two_high = shift(one[1], first, -1)
    return [pack, one, third, two_low, two_high]


def shards(
    start_plan,
    linear_cost,
    price,
    anchor,
    hessian,
    usage_coef,
    crew_limit,
    crew_dual,
    crew_row,
    bundle_of,
    scen_weight,
):
    count, vehicles, n = start_plan.shape
    crews = crew_limit.shape[1]
    bundle_count = anchor.shape[0]
    me = lax.axis_index("scen")
    all_bundles = bundle_of[:, 0]
    my_bundles = lax.dynamic_slice_in_dim(all_bundles, me * count, count)
    all_weights = scen_weight.astype(f32)
    my_weights = lax.dynamic_slice_in_dim(all_weights, me * count, count)

    pad = ((0, 0), (0, CREW_PAD - crews))
    limit = jnp.pad(crew_limit, pad)
    dual = jnp.pad(crew_dual, pad)
    def per_scen(*shape):
        return pl.BlockSpec((1, *shape), lambda s, *_: (s, 0, 0))

    def whole(*shape):
        return pl.BlockSpec(shape, lambda s, *_: (0,) * len(shape))

    params = pltpu.CompilerParams(
        dimension_semantics=("arbitrary",), vmem_limit_bytes=LIMIT
    )
    tall = pltpu.VMEM((count, n, vehicles), f32)
    flat_block = per_scen(vehicles, n)
    pair_block = pl.BlockSpec((2, vehicles, n), lambda s, *_: (s, 0, 0))
    vm = vmem_spec()

    partial, linear, coef_t, row_to_veh, usage = pl.pallas_call(
        first_kernel,
        grid_spec=pltpu.PrefetchScalarGridSpec(
            num_scalar_prefetch=1,
            grid=(count // 2,),
            in_specs=[
                pair_block,
                pair_block,
                pair_block,
                pl.BlockSpec((1, vehicles, n), lambda s, b: (b[2 * s], 0, 0)),
                pl.BlockSpec((1, vehicles, n), lambda s, b: (b[2 * s + 1], 0, 0)),
                pl.BlockSpec((2, n, n), lambda s, *_: (s, 0, 0)),
                whole(vehicles, n),
                whole(count, CREW_PAD),
                whole(1, vehicles),
            ],
            out_specs=[vm] * 5,
            scratch_shapes=[
                pltpu.VMEM((16, 1, vehicles), f32),
                pltpu.VMEM((56, 8, vehicles), f32),
                pltpu.VMEM((2 * n, 2 * n), bf16),
            ],
        ),
        out_shape=[
            tall,
            tall,
            pltpu.VMEM((n, vehicles), f32),
            pltpu.VMEM((CREW_PAD, vehicles), bf16),
            pltpu.VMEM((56, CREW_PAD), f32),
        ],
        compiler_params=params,
        name="first_steps",
    )(
        my_bundles,
        in_hbm(start_plan),
        in_hbm(linear_cost),
        in_hbm(price),
        in_hbm(anchor),
        in_hbm(anchor),
        in_hbm(hessian),
        in_hbm(usage_coef),
        dual,
        crew_row[None, :],
    )

    use_a, use_b = usage_exchange(usage)
    norms = use_a[48:56] + use_b[48:56]
    for _ in range(3):
        partial, usage, dual = pl.pallas_call(
            middle_kernel,
            in_specs=[vm] * 10,
            out_specs=[vm] * 3,
            out_shape=[
                tall,
                pltpu.VMEM((48, CREW_PAD), f32),
                pltpu.VMEM((count, CREW_PAD), f32),
            ],
            input_output_aliases={0: 0},
            scratch_shapes=[
                pltpu.VMEM((48, 1, vehicles), f32),
                pltpu.VMEM((48, 8, vehicles), f32),
                pltpu.VMEM((2 * n, 2 * n), bf16),
            ],
            compiler_params=pltpu.CompilerParams(vmem_limit_bytes=LIMIT),
            name="three_steps",
        )(
            *[
                in_vmem(a)
                for a in (
                    partial,
                    linear,
                    hessian,
                    coef_t,
                    use_a,
                    use_b,
                    norms,
                    limit,
                    dual,
                    row_to_veh,
                )
            ]
        )
        use_a, use_b = usage_exchange(usage)

    me_y, me_x = np.arange(16)[:, None] // 4, np.arange(16)[:, None] % 4
    it_y, it_x = np.arange(16)[None, :] // 4, np.arange(16)[None, :] % 4
    place_a = ((it_x - me_x) % 4) * 4 + (it_y - me_y) % 4
    place_b = ((it_y - me_y) % 4) * 4 + (it_x - me_x) % 4
    here = jnp.arange(16, dtype=jnp.int32) == me
    row_a = jnp.sum(jnp.where(here[:, None], place_a, 0), axis=0)
    row_b = jnp.sum(jnp.where(here[:, None], place_b, 0), axis=0)
    ids = jnp.arange(16, dtype=jnp.int32)
    hot = my_bundles[:, None] == ids[None, :]
    slots = jnp.stack(
        [jnp.sum(jnp.where(hot, row[None, :], 0), axis=1) for row in (row_a, row_b)]
    ).astype(jnp.int32)
    same = my_bundles[:, None] == my_bundles[None, :]
    before = jnp.arange(count)[None, :] < jnp.arange(count)[:, None]
    held = jnp.sum(jnp.where(same & before, my_weights[None, :], 0.0), axis=1)
    factors = jnp.stack(
        [
            my_weights,
            held * my_weights / (held + my_weights),
            1.0 / jnp.maximum(held, 1.0),
        ]
    )
    half = vehicles // 2
    bundle_sums = pltpu.VMEM((bundle_count, half, n), f32)
    quarter = pltpu.VMEM((4, half // 2, n), f32)
    plan, roster, sum_a, sum_b, up_a, down_a, up_b, down_b, spread, dual = pl.pallas_call(
        last_kernel,
        grid_spec=pltpu.PrefetchScalarGridSpec(
            num_scalar_prefetch=2,
            grid=(count,),
            in_specs=[vm] * 10,
            out_specs=[flat_block] + [vm] * 9,
            scratch_shapes=[pltpu.VMEM((32, 1, vehicles), f32)],
        ),
        out_shape=[
            jax.ShapeDtypeStruct((count, vehicles, n), bf16),
            pltpu.VMEM((count, vehicles, n), f32),
            bundle_sums,
            bundle_sums,
            quarter,
            quarter,
            quarter,
            quarter,
            pltpu.VMEM((8, n), f32),
            pltpu.VMEM((count, CREW_PAD), f32),
        ],
        compiler_params=params,
        name="last_step",
    )(
        slots,
        factors,
        *[
            in_vmem(a)
            for a in (
                partial,
                linear,
                hessian,
                coef_t,
                use_a,
                use_b,
                norms,
                limit,
                dual,
                row_to_veh,
            )
        ],
    )

    owners = jnp.arange(all_bundles.shape[0], dtype=jnp.int32) // count

    def weight_table(row):
        device = jnp.sum(jnp.where(owners[:, None] == ids[None, :], row[None, :], 0), axis=1)
        bundle = jnp.sum(jnp.where(all_bundles[:, None] == ids[None, :], row[None, :], 0), axis=1)
        return jnp.sum(
            jnp.where(
                (device[None, None, :] == ids[:, None, None])
                & (bundle[None, None, :] == ids[None, :, None]),
                all_weights[None, None, :],
                0.0,
            ),
            axis=2,
        )

    weights_a = weight_table(row_a)
    weights_b = weight_table(row_b)

    sides = (
        ("x", "y", weights_a, sum_a, up_a, down_a),
        ("y", "x", weights_b, sum_b, up_b, down_b),
    )
    flow = (2, 4, half // 2, n)
    flat = (half, n)
    moved = [(shift(up, f, 1), shift(down, f, -1)) for f, _, _, _, up, down in sides]
    moved = [
        local_call(forward_kernel, w, (sums, up, down), [flow, flow], "forward")
        for (_, _, w, sums, _, _), (up, down) in zip(sides, moved)
    ]
    spreads = [spread] + [m[2] for m in moved]
    moved = [(shift(m[0], side[0], 1), shift(m[1], side[0], -1)) for side, m in zip(sides, moved)]
    moved = [
        local_call(arrive_kernel, w, (sums, up, down), [flat] * 4, "arrive")
        for (_, _, w, sums, _, _), (up, down) in zip(sides, moved)
    ]
    spreads += [m[4] for m in moved]
    moved = [
        (m[0], *[shift(m[by], side[1], by) for by in (1, 2, 3)]) for side, m in zip(sides, moved)
    ]
    moved = [
        local_call(finish_kernel, side[2], m, [flat], "finish") for side, m in zip(sides, moved)
    ]
    spreads += [m[1] for m in moved]
    own_a, own_b = moved[0][0], moved[1][0]
    row_a, row_b = gather_row(own_a, "y"), gather_row(own_b, "x")
    row_a[1], row_b[1], spread = lax.optimization_barrier((row_a[1], row_b[1], sum(spreads)))
    spread = sum(usage_exchange(spread))
    row_a, row_b, spread = lax.optimization_barrier((row_a, row_b, spread))
    near_a, near_b = gather_near(row_a, "x"), gather_near(row_b, "y")
    near_b, spread = lax.optimization_barrier((near_b, spread))
    spread_total = sum_over_scen(spread)
    means = gather_far(*near_a, "x") + gather_far(*near_b, "y")
    entries = vehicles * lax.axis_size("veh") * n

    each = 2
    new_price, gap = pl.pallas_call(
        price_kernel,
        grid_spec=pltpu.PrefetchScalarGridSpec(
            num_scalar_prefetch=1,
            grid=(count // each,),
            in_specs=[vm, pair_block] + [vm] * 12,
            out_specs=[pair_block, whole(1, 1)],
        ),
        out_shape=[
            jax.ShapeDtypeStruct((count, vehicles, n), bf16),
            jax.ShapeDtypeStruct((1, 1), f32),
        ],
        compiler_params=params,
        name="new_price",
    )(
        slots,
        in_vmem(roster),
        in_hbm(price),
        in_vmem(spread_total),
        in_vmem((all_weights * entries)[None, :]),
        *[in_vmem(m) for m in means],
    )

    own_mean = jnp.concatenate([own_a, own_b], axis=0)
    return (plan, new_price, own_mean.astype(bf16)[None], dual[:, :crews], gap[0, 0])


def solution(mesh):
    return jax.shard_map(
        shards,
        mesh=mesh,
        in_specs=(
            P("scen", "veh", None),
            P("scen", "veh", None),
            P("scen", "veh", None),
            P(None, "veh", None),
            P("scen", None, None),
            P("veh", None),
            P("scen", None),
            P("scen", None),
            P("veh"),
            P(),
            P(),
        ),
        out_specs=(
            P("scen", "veh", None),
            P("scen", "veh", None),
            P("scen", "veh", None),
            P("scen", None),
            P(),
        ),
        check_vma=False,
    )
```

```python
import functools

import jax
import jax.numpy as jnp
import numpy as np
from jax import lax
from jax.experimental import pallas as pl
from jax.experimental.pallas import tpu as pltpu
from jax.sharding import PartitionSpec as P

ITERS = 12
penalty = 1.0
step_size = 0.02
dual_step = 0.02
keep = 1.0 - step_size * penalty
CREW_PAD = 384
LIMIT = 14 * 1024 * 1024
bf16 = jnp.bfloat16
f32 = jnp.float32

PAIR_A = {0: 1, 1: 0, 2: 3, 3: 2}
PAIR_B = {0: 3, 3: 0, 1: 2, 2: 1}


def split3(value):
    hi = value.astype(bf16)
    rest = value - hi.astype(f32)
    mid = rest.astype(bf16)
    low = (rest - mid.astype(f32)).astype(bf16)
    return jnp.concatenate([hi, mid, low], axis=0)


def exact_dot(left, right):
    rows = left.shape[0]
    out = jnp.dot(split3(left), right, preferred_element_type=f32)
    return out[:rows] + out[rows : 2 * rows] + out[2 * rows :]


def folded(value):
    return jnp.sum(value.reshape(-1, 8, value.shape[1]), axis=0)


def used_dot(used, row_to_veh):
    flat = jnp.sum(used, axis=1)
    rows = flat.shape[0]
    out = lax.dot_general(
        split3(flat), row_to_veh, (((1,), (1,)), ((), ())), preferred_element_type=f32
    )
    return out[:rows] + out[rows : 2 * rows] + out[2 * rows :]


def first_kernel(
    bundles,
    start_ref,
    cost_ref,
    price_ref,
    anchor_0,
    anchor_1,
    hess_ref,
    coef_ref,
    dual_ref,
    row_ref,
    partial_ref,
    linear_ref,
    coef_t_ref,
    row_to_veh,
    usage_ref,
    crew_scr,
    used_scr,
    block_scr,
):
    step = pl.program_id(0)
    count = pl.num_programs(0)
    n = hess_ref.shape[-1]

    @pl.when(step == 0)
    def _():
        block_scr[...] = jnp.zeros_like(block_scr)
        ids = lax.broadcasted_iota(jnp.int32, row_to_veh.shape, 0)
        row_to_veh[...] = (ids == row_ref[...]).astype(f32).astype(bf16)
        crew_scr[:, 0, :] = step_size * exact_dot(dual_ref[...], row_to_veh[...])
        used_scr[48:56] = jnp.zeros_like(used_scr[48:56])
        c = coef_ref[...].astype(f32).T
        coef_t_ref[...] = c
        used_scr[48] = folded(c * c)

    block_scr[0:n, 0:n] = hess_ref[0]
    block_scr[n:, n:] = hess_ref[1]
    both = block_scr[...]
    c = coef_t_ref[...]
    s = 2 * step
    xs = []
    for i, anchor_ref in enumerate((anchor_0, anchor_1)):
        linear = step_size * (
            cost_ref[i].astype(f32) + price_ref[i].astype(f32) - penalty * anchor_ref[0].astype(f32)
        )
        linear_ref[s + i] = linear.T
        x = start_ref[i].T.astype(f32)
        used_scr[s + i] = folded(c * x)
        xs.append(x)
    for k in (1, 2):
        stacked = jnp.concatenate([x.astype(bf16) for x in xs], axis=0)
        curve = jnp.dot(both, stacked, preferred_element_type=f32)
        for i in range(2):
            x = (keep * xs[i] - linear_ref[s + i]) - step_size * curve[i * n : (i + 1) * n]
            if k < 2:
                x = x - crew_scr[s + i] * c
            used_scr[16 * k + s + i] = folded(c * x)
            xs[i] = x
    for i in range(2):
        partial_ref[s + i] = xs[i]

    @pl.when(step == count - 1)
    def _():
        usage_ref[...] = used_dot(used_scr[...], row_to_veh[...])


def summed(a, b, c, d):
    return (a[...] + c[...]) + (b[...] + d[...])


def crew_update(usage, norms, limit, dual):
    one = jnp.maximum(dual + dual_step * (usage[0:16] - limit), 0.0)
    third = usage[32:48] - step_size * one * norms
    two = jnp.maximum(one + dual_step * (usage[16:32] - limit), 0.0)
    three = jnp.maximum(two + dual_step * (third - limit), 0.0)
    return one, two, three


def middle_kernel(
    partial_ref,
    linear_ref,
    hess_ref,
    coef_t_ref,
    use_0,
    use_1,
    use_2,
    use_3,
    norms_ref,
    limit_ref,
    dual_ref,
    row_to_veh,
    next_ref,
    usage_ref,
    new_dual_ref,
    crew_scr,
    used_scr,
    block_scr,
):
    count = partial_ref.shape[0]
    n = hess_ref.shape[-1]
    one, two, three = crew_update(
        summed(use_0, use_1, use_2, use_3)[0:48], norms_ref[0:1], limit_ref[...], dual_ref[...]
    )
    new_dual_ref[...] = three
    crew_scr[:, 0, :] = step_size * exact_dot(
        jnp.concatenate([one, two, three], axis=0), row_to_veh[...]
    )
    block_scr[...] = jnp.zeros_like(block_scr)

    def two_scenarios(pair, carry):
        s = 2 * pair
        block_scr[0:n, 0:n] = hess_ref[s]
        block_scr[n:, n:] = hess_ref[s + 1]
        both = block_scr[...]
        c = coef_t_ref[...]
        xs = [partial_ref[s + i] - crew_scr[s + i] * c for i in range(2)]
        for k in (1, 2, 3):
            stacked = jnp.concatenate([x.astype(bf16) for x in xs], axis=0)
            curve = jnp.dot(both, stacked, preferred_element_type=f32)
            for i in range(2):
                x = (keep * xs[i] - linear_ref[s + i]) - step_size * curve[i * n : (i + 1) * n]
                if k < 3:
                    x = x - crew_scr[16 * k + s + i] * c
                used_scr[16 * (k - 1) + s + i] = folded(c * x)
                xs[i] = x
        for i in range(2):
            next_ref[s + i] = xs[i]
        return carry

    lax.fori_loop(0, count // 2, two_scenarios, 0)
    usage_ref[...] = used_dot(used_scr[...], row_to_veh[...])


def last_kernel(
    slots,
    factors,
    partial_ref,
    linear_ref,
    hess_ref,
    coef_t_ref,
    use_0,
    use_1,
    use_2,
    use_3,
    norms_ref,
    limit_ref,
    dual_ref,
    row_to_veh,
    plan_ref,
    roster_ref,
    sum_a,
    sum_b,
    send_au,
    send_ad,
    send_bu,
    send_bd,
    spread_ref,
    new_dual_ref,
    crew_scr,
):
    s = pl.program_id(0)
    count = pl.num_programs(0)
    rows = sum_a.shape[1]

    @pl.when(s == 0)
    def _():
        one, two, three = crew_update(
            summed(use_0, use_1, use_2, use_3)[0:48], norms_ref[0:1], limit_ref[...], dual_ref[...]
        )
        new_dual_ref[...] = three
        crew_scr[:, 0, :] = step_size * exact_dot(
            jnp.concatenate([one, two], axis=0), row_to_veh[...]
        )
        sum_a[...] = jnp.zeros_like(sum_a)
        sum_b[...] = jnp.zeros_like(sum_b)
        spread_ref[...] = jnp.zeros_like(spread_ref)

    c = coef_t_ref[...]
    x = partial_ref[s] - crew_scr[s] * c
    curve = jnp.dot(hess_ref[s], x.astype(bf16), preferred_element_type=f32)
    x = (keep * x - linear_ref[s]) - step_size * curve - crew_scr[16 + s] * c
    roster_ref[s] = x.T

    weight, merge, inverse = factors[0, s], factors[1, s], factors[2, s]
    part = 112
    spread = jnp.zeros((8, 128), f32)
    for side, sums in enumerate((sum_a, sum_b)):
        slot = slots[side, s]
        for start in range(0, rows, part):
            here = pl.ds(side * rows + start, part)
            x = roster_ref[s, here, :]
            plan_ref[0, here, :] = x.astype(bf16)
            held = sums[slot, start : start + part, :]
            gap = held * inverse - x
            spread = spread + merge * folded(gap * gap)
            sums[slot, start : start + part, :] = held + weight * x
    spread_ref[...] += spread

    @pl.when(s == count - 1)
    def _():
        for sums, up, down in ((sum_a, send_au, send_ad), (sum_b, send_bu, send_bd)):
            for k in range(4):
                up[k] = sums[8 + k, : rows // 2, :]
                down[k] = sums[8 + k, rows // 2 :, :]


def merge_into(total, weight, other, other_weight):
    weight = jnp.full((8, 128), weight, f32)
    other_weight = jnp.full((8, 128), other_weight, f32)
    both = weight + other_weight
    factor = jnp.where(both > 0, weight * other_weight / jnp.maximum(both, 1.0), 0.0)
    shape = total.shape
    total8, other8 = total.reshape(-1, 8, 128), other.reshape(-1, 8, 128)
    gap = total8 * (1.0 / jnp.maximum(weight, 1.0)) - other8 * (1.0 / jnp.maximum(other_weight, 1.0))
    return total + other, factor * jnp.sum(gap * gap, axis=0)


def forward_kernel(weights, sums, up_in, down_in, up_out, down_out, spread_ref):
    rows = sums.shape[1] // 2
    spread = jnp.zeros((8, 128), f32)
    for k in range(4):
        total, more = merge_into(sums[4 + k, :rows, :], weights[0, 4 + k], up_in[k], weights[12, 4 + k])
        spread += more
        up_out[0, k] = total
        up_out[1, k] = sums[4 + k, rows:, :]
        down_out[0, k] = sums[12 + k, :rows, :]
        total, more = merge_into(
            sums[12 + k, rows:, :], weights[0, 12 + k], down_in[k], weights[4, 12 + k]
        )
        spread += more
        down_out[1, k] = total
    spread_ref[...] = spread


def arrive_kernel(weights, sums, up_in, down_in, own, out_1, out_2, out_3, spread_ref):
    rows = sums.shape[1] // 2
    spread = jnp.zeros((8, 128), f32)
    for k, out in enumerate((own, out_1, out_2, out_3)):
        w0, w1, w2, w3 = (weights[4 * e, k] for e in range(4))
        for half in range(2):
            here = slice(half * rows, (half + 1) * rows)
            w_up, w_down = (w3 + w2, w1) if half == 0 else (w3, w1 + w2)
            total, more = merge_into(sums[k, here, :], w0, up_in[half, k], w_up)
            spread += more
            total, more = merge_into(total, w0 + w_up, down_in[half, k], w_down)
            spread += more
            out[here, :] = total
    spread_ref[...] = spread


def finish_kernel(weights, own, in_1, in_2, in_3, mean_ref, spread_ref):
    line = [sum(weights[4 * e + j, 0] for e in range(4)) for j in range(4)]
    total, weight = own[...], line[0]
    spread = jnp.zeros((8, 128), f32)
    for by, part in ((1, in_1), (3, in_3), (2, in_2)):
        total, more = merge_into(total, weight, part[...], line[4 - by])
        spread += more
        weight = weight + line[4 - by]
    mean_ref[...] = total / jnp.full((8, 128), weight, f32)[0:1]
    spread_ref[...] = spread


def price_kernel(slots, roster_ref, price_ref, spread_ref, weight_ref, *refs):
    means, out_ref, gap_ref = refs[:10], refs[10], refs[11]
    each = price_ref.shape[0]
    rows = means[3].shape[1]

    @pl.when(pl.program_id(0) == 0)
    def _():
        spread = jnp.sum(spread_ref[...], keepdims=True)
        gap_ref[...] = jnp.sqrt(spread / jnp.sum(weight_ref[...], keepdims=True))

    for i in range(each):
        s = pl.program_id(0) * each + i
        for side in range(2):
            slot = slots[side, s]
            first, second = slot // 4, slot % 4
            pack, one, third, two_low, two_high = means[side * 5 : side * 5 + 5]
            for k in range(4):

                @pl.when(first == k)
                def _():
                    for half in range(2):
                        if k == 2:
                            mean = (two_low, two_high)[half][second]
                        else:
                            mean = (pack, one, None, third)[k][half, second]
                        here = pl.ds((side * 2 + half) * rows, rows)
                        deviation = roster_ref[s, here, :] - mean
                        out_ref[i, here, :] = (
                            price_ref[i, here, :].astype(f32) + penalty * deviation
                        ).astype(bf16)


def veh_pairs(kind):
    if kind == "core":
        return [(i, i ^ 1) for i in range(8)]
    return [(z * 2 + c, kind[z] * 2 + c) for z in range(4) for c in range(2)]


def scen_pairs(pair, axis):
    out = []
    for y in range(4):
        for x in range(4):
            to = (y * 4 + pair[x]) if axis == "x" else (pair[y] * 4 + x)
            out.append((y * 4 + x, to))
    return out


def usage_exchange(value):
    value = value + lax.ppermute(value, "veh", veh_pairs("core"))
    turns = [
        lax.ppermute(value, "veh", veh_pairs({z: (z + by) % 4 for z in range(4)}))
        for by in (1, 3, 2)
    ]
    return [value, turns[0], turns[2], turns[1]]


def spread_over_veh(value):
    for kind in ("core", PAIR_A, PAIR_B):
        value = value + lax.ppermute(value, "veh", veh_pairs(kind))
    return value


def sum_over_scen(value):
    for axis in ("x", "y"):
        for pair in (PAIR_A, PAIR_B):
            value = value + lax.ppermute(value, "scen", scen_pairs(pair, axis))
    return value


def shift(value, axis, by):
    pairs = []
    for y in range(4):
        for x in range(4):
            to = (y * 4 + (x + by) % 4) if axis == "x" else (((y + by) % 4) * 4 + x)
            pairs.append((y * 4 + x, to))
    return lax.ppermute(value, "scen", pairs)


def vmem_spec():
    return pl.BlockSpec(memory_space=pltpu.VMEM)


def in_vmem(value):
    return pltpu.with_memory_space_constraint(value, pltpu.VMEM)


def in_hbm(value):
    return pltpu.with_memory_space_constraint(value, pltpu.HBM)


def local_call(body, weights, arrays, out_shapes, name):
    return pl.pallas_call(
        body,
        in_specs=[pl.BlockSpec(memory_space=pltpu.SMEM)] + [vmem_spec()] * len(arrays),
        out_specs=[vmem_spec()] * (len(out_shapes) + 1),
        out_shape=[pltpu.VMEM(shape, f32) for shape in out_shapes] + [pltpu.VMEM((8, 128), f32)],
        compiler_params=pltpu.CompilerParams(vmem_limit_bytes=LIMIT),
        name=name,
    )(weights, *[in_vmem(a) for a in arrays])


def gather_row(own, second):
    return {0: own, **{by: shift(own, second, -by) for by in (1, 3, 2)}}


def gather_pack(row):
    rows = row[0].shape[0] // 2
    return jnp.stack([row[k].reshape(2, rows, -1) for k in range(4)], axis=1)


def gather_near(pack, first):
    return pack, shift(pack, first, -1), shift(pack, first, 1)


def gather_far(pack, one, third, first):
    two_low = shift(third[0], first, 1)
    two_high = shift(one[1], first, -1)
    return [pack, one, third, two_low, two_high]


def shards(
    start_plan,
    linear_cost,
    price,
    anchor,
    hessian,
    usage_coef,
    crew_limit,
    crew_dual,
    crew_row,
    bundle_of,
    scen_weight,
):
    count, vehicles, n = start_plan.shape
    crews = crew_limit.shape[1]
    bundle_count = anchor.shape[0]
    me = lax.axis_index("scen")
    all_bundles = bundle_of[:, 0]
    my_bundles = lax.dynamic_slice_in_dim(all_bundles, me * count, count)
    all_weights = scen_weight.astype(f32)
    my_weights = lax.dynamic_slice_in_dim(all_weights, me * count, count)

    pad = ((0, 0), (0, CREW_PAD - crews))
    limit = jnp.pad(crew_limit, pad)
    dual = jnp.pad(crew_dual, pad)
    def per_scen(*shape):
        return pl.BlockSpec((1, *shape), lambda s, *_: (s, 0, 0))

    def whole(*shape):
        return pl.BlockSpec(shape, lambda s, *_: (0,) * len(shape))

    params = pltpu.CompilerParams(
        dimension_semantics=("arbitrary",), vmem_limit_bytes=LIMIT
    )
    tall = pltpu.VMEM((count, n, vehicles), f32)
    flat_block = per_scen(vehicles, n)
    pair_block = pl.BlockSpec((2, vehicles, n), lambda s, *_: (s, 0, 0))
    vm = vmem_spec()

    partial, linear, coef_t, row_to_veh, usage = pl.pallas_call(
        first_kernel,
        grid_spec=pltpu.PrefetchScalarGridSpec(
            num_scalar_prefetch=1,
            grid=(count // 2,),
            in_specs=[
                pair_block,
                pair_block,
                pair_block,
                pl.BlockSpec((1, vehicles, n), lambda s, b: (b[2 * s], 0, 0)),
                pl.BlockSpec((1, vehicles, n), lambda s, b: (b[2 * s + 1], 0, 0)),
                pl.BlockSpec((2, n, n), lambda s, *_: (s, 0, 0)),
                whole(vehicles, n),
                whole(count, CREW_PAD),
                whole(1, vehicles),
            ],
            out_specs=[vm] * 5,
            scratch_shapes=[
                pltpu.VMEM((16, 1, vehicles), f32),
                pltpu.VMEM((56, 8, vehicles), f32),
                pltpu.VMEM((2 * n, 2 * n), bf16),
            ],
        ),
        out_shape=[
            tall,
            tall,
            pltpu.VMEM((n, vehicles), f32),
            pltpu.VMEM((CREW_PAD, vehicles), bf16),
            pltpu.VMEM((56, CREW_PAD), f32),
        ],
        compiler_params=params,
        name="first_steps",
    )(
        my_bundles,
        in_hbm(start_plan),
        in_hbm(linear_cost),
        in_hbm(price),
        in_hbm(anchor),
        in_hbm(anchor),
        in_hbm(hessian),
        in_hbm(usage_coef),
        dual,
        crew_row[None, :],
    )

    use = usage_exchange(usage)
    norms = summed(*[u[48:56] for u in use])
    for _ in range(3):
        partial, usage, dual = pl.pallas_call(
            middle_kernel,
            in_specs=[vm] * 12,
            out_specs=[vm] * 3,
            out_shape=[
                tall,
                pltpu.VMEM((48, CREW_PAD), f32),
                pltpu.VMEM((count, CREW_PAD), f32),
            ],
            input_output_aliases={0: 0},
            scratch_shapes=[
                pltpu.VMEM((48, 1, vehicles), f32),
                pltpu.VMEM((48, 8, vehicles), f32),
                pltpu.VMEM((2 * n, 2 * n), bf16),
            ],
            compiler_params=pltpu.CompilerParams(vmem_limit_bytes=LIMIT),
            name="three_steps",
        )(
            *[
                in_vmem(a)
                for a in (
                    partial,
                    linear,
                    hessian,
                    coef_t,
                    *use,
                    norms,
                    limit,
                    dual,
                    row_to_veh,
                )
            ]
        )
        use = usage_exchange(usage)

    me_y, me_x = np.arange(16)[:, None] // 4, np.arange(16)[:, None] % 4
    it_y, it_x = np.arange(16)[None, :] // 4, np.arange(16)[None, :] % 4
    place_a = ((it_x - me_x) % 4) * 4 + (it_y - me_y) % 4
    place_b = ((it_y - me_y) % 4) * 4 + (it_x - me_x) % 4
    here = jnp.arange(16, dtype=jnp.int32) == me
    row_a = jnp.sum(jnp.where(here[:, None], place_a, 0), axis=0)
    row_b = jnp.sum(jnp.where(here[:, None], place_b, 0), axis=0)
    ids = jnp.arange(16, dtype=jnp.int32)
    hot = my_bundles[:, None] == ids[None, :]
    slots = jnp.stack(
        [jnp.sum(jnp.where(hot, row[None, :], 0), axis=1) for row in (row_a, row_b)]
    ).astype(jnp.int32)
    same = my_bundles[:, None] == my_bundles[None, :]
    before = jnp.arange(count)[None, :] < jnp.arange(count)[:, None]
    held = jnp.sum(jnp.where(same & before, my_weights[None, :], 0.0), axis=1)
    factors = jnp.stack(
        [
            my_weights,
            held * my_weights / (held + my_weights),
            1.0 / jnp.maximum(held, 1.0),
        ]
    )
    half = vehicles // 2
    bundle_sums = pltpu.VMEM((bundle_count, half, n), f32)
    quarter = pltpu.VMEM((4, half // 2, n), f32)
    plan, roster, sum_a, sum_b, up_a, down_a, up_b, down_b, spread, dual = pl.pallas_call(
        last_kernel,
        grid_spec=pltpu.PrefetchScalarGridSpec(
            num_scalar_prefetch=2,
            grid=(count,),
            in_specs=[vm] * 12,
            out_specs=[flat_block] + [vm] * 9,
            scratch_shapes=[pltpu.VMEM((32, 1, vehicles), f32)],
        ),
        out_shape=[
            jax.ShapeDtypeStruct((count, vehicles, n), bf16),
            pltpu.VMEM((count, vehicles, n), f32),
            bundle_sums,
            bundle_sums,
            quarter,
            quarter,
            quarter,
            quarter,
            pltpu.VMEM((8, n), f32),
            pltpu.VMEM((count, CREW_PAD), f32),
        ],
        compiler_params=params,
        name="last_step",
    )(
        slots,
        factors,
        *[
            in_vmem(a)
            for a in (
                partial,
                linear,
                hessian,
                coef_t,
                *use,
                norms,
                limit,
                dual,
                row_to_veh,
            )
        ],
    )

    owners = jnp.arange(all_bundles.shape[0], dtype=jnp.int32) // count

    def weight_table(row):
        device = jnp.sum(jnp.where(owners[:, None] == ids[None, :], row[None, :], 0), axis=1)
        bundle = jnp.sum(jnp.where(all_bundles[:, None] == ids[None, :], row[None, :], 0), axis=1)
        return jnp.sum(
            jnp.where(
                (device[None, None, :] == ids[:, None, None])
                & (bundle[None, None, :] == ids[None, :, None]),
                all_weights[None, None, :],
                0.0,
            ),
            axis=2,
        )

    weights_a = weight_table(row_a)
    weights_b = weight_table(row_b)

    sides = (
        ("x", "y", weights_a, sum_a, up_a, down_a),
        ("y", "x", weights_b, sum_b, up_b, down_b),
    )
    flow = (2, 4, half // 2, n)
    flat = (half, n)
    moved = [(shift(up, f, 1), shift(down, f, -1)) for f, _, _, _, up, down in sides]
    moved = [
        local_call(forward_kernel, w, (sums, up, down), [flow, flow], "forward")
        for (_, _, w, sums, _, _), (up, down) in zip(sides, moved)
    ]
    spreads = [spread] + [m[2] for m in moved]
    moved = [(shift(m[0], side[0], 1), shift(m[1], side[0], -1)) for side, m in zip(sides, moved)]
    moved = [
        local_call(arrive_kernel, w, (sums, up, down), [flat] * 4, "arrive")
        for (_, _, w, sums, _, _), (up, down) in zip(sides, moved)
    ]
    spreads += [m[4] for m in moved]
    moved = [
        (m[0], *[shift(m[by], side[1], by) for by in (1, 2, 3)]) for side, m in zip(sides, moved)
    ]
    moved = [
        local_call(finish_kernel, side[2], m, [flat], "finish") for side, m in zip(sides, moved)
    ]
    spreads += [m[1] for m in moved]
    own_a, own_b = moved[0][0], moved[1][0]
    row_a, row_b = gather_row(own_a, "y"), gather_row(own_b, "x")
    pack_a, pack_b = gather_pack(row_a), gather_pack(row_b)
    pack_a, pack_b, spread = lax.optimization_barrier((pack_a, pack_b, sum(spreads)))
    near_a, near_b = gather_near(pack_a, "x"), gather_near(pack_b, "y")
    spread = spread_over_veh(spread)
    near_b, spread = lax.optimization_barrier((near_b, spread))
    spread_total = sum_over_scen(spread)
    means = gather_far(*near_a, "x") + gather_far(*near_b, "y")
    entries = vehicles * lax.axis_size("veh") * n

    each = 2
    new_price, gap = pl.pallas_call(
        price_kernel,
        grid_spec=pltpu.PrefetchScalarGridSpec(
            num_scalar_prefetch=1,
            grid=(count // each,),
            in_specs=[vm, pair_block] + [vm] * 12,
            out_specs=[pair_block, whole(1, 1)],
        ),
        out_shape=[
            jax.ShapeDtypeStruct((count, vehicles, n), bf16),
            jax.ShapeDtypeStruct((1, 1), f32),
        ],
        compiler_params=params,
        name="new_price",
    )(
        slots,
        in_vmem(roster),
        in_hbm(price),
        in_vmem(spread_total),
        in_vmem((all_weights * entries)[None, :]),
        *[in_vmem(m) for m in means],
    )

    own_mean = jnp.concatenate([own_a, own_b], axis=0)
    return (plan, new_price, own_mean.astype(bf16)[None], dual[:, :crews], gap[0, 0])


def solution(mesh):
    return jax.shard_map(
        shards,
        mesh=mesh,
        in_specs=(
            P("scen", "veh", None),
            P("scen", "veh", None),
            P("scen", "veh", None),
            P(None, "veh", None),
            P("scen", None, None),
            P("veh", None),
            P("scen", None),
            P("scen", None),
            P("veh"),
            P(),
            P(),
        ),
        out_specs=(
            P("scen", "veh", None),
            P("scen", "veh", None),
            P("scen", "veh", None),
            P("scen", None),
            P(),
        ),
        check_vma=False,
    )
```

```python
import functools

import jax
import jax.numpy as jnp
import numpy as np
from jax import lax
from jax.experimental import pallas as pl
from jax.experimental.pallas import tpu as pltpu
from jax.sharding import PartitionSpec as P

ITERS = 12
penalty = 1.0
step_size = 0.02
dual_step = 0.02
keep = 1.0 - step_size * penalty
CREW_PAD = 384
LIMIT = 14 * 1024 * 1024
bf16 = jnp.bfloat16
f32 = jnp.float32

PAIR_A = {0: 1, 1: 0, 2: 3, 3: 2}
PAIR_B = {0: 3, 3: 0, 1: 2, 2: 1}


def split3(value):
    hi = value.astype(bf16)
    rest = value - hi.astype(f32)
    mid = rest.astype(bf16)
    low = (rest - mid.astype(f32)).astype(bf16)
    return jnp.concatenate([hi, mid, low], axis=0)


def exact_dot(left, right):
    rows = left.shape[0]
    out = jnp.dot(split3(left), right, preferred_element_type=f32)
    return out[:rows] + out[rows : 2 * rows] + out[2 * rows :]


def folded(value):
    return jnp.sum(value.reshape(-1, 8, value.shape[1]), axis=0)


def used_dot(used, row_to_veh):
    flat = jnp.sum(used, axis=1)
    rows = flat.shape[0]
    out = lax.dot_general(
        split3(flat), row_to_veh, (((1,), (1,)), ((), ())), preferred_element_type=f32
    )
    return out[:rows] + out[rows : 2 * rows] + out[2 * rows :]


def first_kernel(
    bundles,
    start_ref,
    cost_ref,
    price_ref,
    anchor_0,
    anchor_1,
    hess_ref,
    coef_ref,
    dual_ref,
    row_ref,
    partial_ref,
    linear_ref,
    coef_t_ref,
    row_to_veh,
    usage_ref,
    crew_scr,
    used_scr,
    block_scr,
    dual_scr,
):
    step = pl.program_id(0)
    count = pl.num_programs(0)
    n = hess_ref.shape[-1]

    @pl.when(step == 0)
    def _():
        block_scr[...] = jnp.zeros_like(block_scr)
        ids = lax.broadcasted_iota(jnp.int32, row_to_veh.shape, 0)
        row_to_veh[...] = (ids == row_ref[...]).astype(f32).astype(bf16)
        dual_scr[...] = jnp.zeros_like(dual_scr)
        dual_scr[:, : dual_ref.shape[1]] = dual_ref[...]
        crew_scr[:, 0, :] = step_size * exact_dot(dual_scr[...], row_to_veh[...])
        used_scr[48:56] = jnp.zeros_like(used_scr[48:56])
        c = coef_ref[...].astype(f32).T
        coef_t_ref[...] = c
        used_scr[48] = folded(c * c)

    block_scr[0:n, 0:n] = hess_ref[0]
    block_scr[n:, n:] = hess_ref[1]
    both = block_scr[...]
    c = coef_t_ref[...]
    s = 2 * step
    xs = []
    for i, anchor_ref in enumerate((anchor_0, anchor_1)):
        linear = step_size * (
            cost_ref[i].astype(f32) + price_ref[i].astype(f32) - penalty * anchor_ref[0].astype(f32)
        )
        linear_ref[s + i] = linear.T
        x = start_ref[i].T.astype(f32)
        used_scr[s + i] = folded(c * x)
        xs.append(x)
    for k in (1, 2):
        stacked = jnp.concatenate([x.astype(bf16) for x in xs], axis=0)
        curve = jnp.dot(both, stacked, preferred_element_type=f32)
        for i in range(2):
            x = (keep * xs[i] - linear_ref[s + i]) - step_size * curve[i * n : (i + 1) * n]
            if k < 2:
                x = x - crew_scr[s + i] * c
            used_scr[16 * k + s + i] = folded(c * x)
            xs[i] = x
    for i in range(2):
        partial_ref[s + i] = xs[i]

    @pl.when(step == count - 1)
    def _():
        usage_ref[...] = used_dot(used_scr[...], row_to_veh[...])


def summed(a, b, c, d):
    return (a[...] + c[...]) + (b[...] + d[...])


def crew_update(usage, norms, limit, dual):
    one = jnp.maximum(dual + dual_step * (usage[0:16] - limit), 0.0)
    third = usage[32:48] - step_size * one * norms
    two = jnp.maximum(one + dual_step * (usage[16:32] - limit), 0.0)
    three = jnp.maximum(two + dual_step * (third - limit), 0.0)
    return one, two, three


def middle_kernel(
    partial_ref,
    linear_ref,
    hess_ref,
    coef_t_ref,
    use_0,
    use_1,
    use_2,
    use_3,
    norms_ref,
    limit_ref,
    dual_ref,
    row_to_veh,
    next_ref,
    usage_ref,
    new_dual_ref,
    crew_scr,
    used_scr,
    block_scr,
):
    count = partial_ref.shape[0]
    n = hess_ref.shape[-1]
    one, two, three = crew_update(
        summed(use_0, use_1, use_2, use_3)[0:48], norms_ref[0:1], limit_ref[...], dual_ref[...]
    )
    new_dual_ref[...] = three
    crew_scr[:, 0, :] = step_size * exact_dot(
        jnp.concatenate([one, two, three], axis=0), row_to_veh[...]
    )
    block_scr[...] = jnp.zeros_like(block_scr)

    def two_scenarios(pair, carry):
        s = 2 * pair
        block_scr[0:n, 0:n] = hess_ref[s]
        block_scr[n:, n:] = hess_ref[s + 1]
        both = block_scr[...]
        c = coef_t_ref[...]
        xs = [partial_ref[s + i] - crew_scr[s + i] * c for i in range(2)]
        for k in (1, 2, 3):
            stacked = jnp.concatenate([x.astype(bf16) for x in xs], axis=0)
            curve = jnp.dot(both, stacked, preferred_element_type=f32)
            for i in range(2):
                x = (keep * xs[i] - linear_ref[s + i]) - step_size * curve[i * n : (i + 1) * n]
                if k < 3:
                    x = x - crew_scr[16 * k + s + i] * c
                used_scr[16 * (k - 1) + s + i] = folded(c * x)
                xs[i] = x
        for i in range(2):
            next_ref[s + i] = xs[i]
        return carry

    lax.fori_loop(0, count // 2, two_scenarios, 0)
    usage_ref[...] = used_dot(used_scr[...], row_to_veh[...])


def last_kernel(
    slots,
    factors,
    partial_ref,
    linear_ref,
    hess_ref,
    coef_t_ref,
    use_0,
    use_1,
    use_2,
    use_3,
    norms_ref,
    limit_ref,
    dual_ref,
    row_to_veh,
    plan_ref,
    roster_ref,
    sum_a,
    sum_b,
    send_au,
    send_ad,
    send_bu,
    send_bd,
    spread_ref,
    new_dual_ref,
    crew_scr,
):
    s = pl.program_id(0)
    count = pl.num_programs(0)
    rows = sum_a.shape[1]

    @pl.when(s == 0)
    def _():
        one, two, three = crew_update(
            summed(use_0, use_1, use_2, use_3)[0:48], norms_ref[0:1], limit_ref[...], dual_ref[...]
        )
        new_dual_ref[...] = three
        crew_scr[:, 0, :] = step_size * exact_dot(
            jnp.concatenate([one, two], axis=0), row_to_veh[...]
        )
        sum_a[...] = jnp.zeros_like(sum_a)
        sum_b[...] = jnp.zeros_like(sum_b)
        spread_ref[...] = jnp.zeros_like(spread_ref)

    c = coef_t_ref[...]
    x = partial_ref[s] - crew_scr[s] * c
    curve = jnp.dot(hess_ref[s], x.astype(bf16), preferred_element_type=f32)
    x = (keep * x - linear_ref[s]) - step_size * curve - crew_scr[16 + s] * c
    roster_ref[s] = x.T

    weight, merge, inverse = factors[0, s], factors[1, s], factors[2, s]
    part = 112
    spread = jnp.zeros((8, 128), f32)
    for side, sums in enumerate((sum_a, sum_b)):
        slot = slots[side, s]
        for start in range(0, rows, part):
            here = pl.ds(side * rows + start, part)
            x = roster_ref[s, here, :]
            plan_ref[0, here, :] = x.astype(bf16)
            held = sums[slot, start : start + part, :]
            gap = held * inverse - x
            spread = spread + merge * folded(gap * gap)
            sums[slot, start : start + part, :] = held + weight * x
    spread_ref[...] += spread

    @pl.when(s == count - 1)
    def _():
        for sums, up, down in ((sum_a, send_au, send_ad), (sum_b, send_bu, send_bd)):
            for k in range(4):
                up[k] = sums[8 + k, : rows // 2, :]
                down[k] = sums[8 + k, rows // 2 :, :]


def merge_into(total, weight, other, other_weight):
    weight = jnp.full((8, 128), weight, f32)
    other_weight = jnp.full((8, 128), other_weight, f32)
    both = weight + other_weight
    factor = jnp.where(both > 0, weight * other_weight / jnp.maximum(both, 1.0), 0.0)
    shape = total.shape
    total8, other8 = total.reshape(-1, 8, 128), other.reshape(-1, 8, 128)
    gap = total8 * (1.0 / jnp.maximum(weight, 1.0)) - other8 * (1.0 / jnp.maximum(other_weight, 1.0))
    return total + other, factor * jnp.sum(gap * gap, axis=0)


def forward_kernel(weights, sums, up_in, down_in, up_out, down_out, spread_ref):
    rows = sums.shape[1] // 2
    spread = jnp.zeros((8, 128), f32)
    for k in range(4):
        total, more = merge_into(sums[4 + k, :rows, :], weights[0, 4 + k], up_in[k], weights[12, 4 + k])
        spread += more
        up_out[0, k] = total
        up_out[1, k] = sums[4 + k, rows:, :]
        down_out[0, k] = sums[12 + k, :rows, :]
        total, more = merge_into(
            sums[12 + k, rows:, :], weights[0, 12 + k], down_in[k], weights[4, 12 + k]
        )
        spread += more
        down_out[1, k] = total
    spread_ref[...] = spread


def arrive_kernel(weights, sums, up_in, down_in, own, out_1, out_2, out_3, spread_ref):
    rows = sums.shape[1] // 2
    spread = jnp.zeros((8, 128), f32)
    for k, out in enumerate((own, out_1, out_2, out_3)):
        w0, w1, w2, w3 = (weights[4 * e, k] for e in range(4))
        for half in range(2):
            here = slice(half * rows, (half + 1) * rows)
            w_up, w_down = (w3 + w2, w1) if half == 0 else (w3, w1 + w2)
            total, more = merge_into(sums[k, here, :], w0, up_in[half, k], w_up)
            spread += more
            total, more = merge_into(total, w0 + w_up, down_in[half, k], w_down)
            spread += more
            out[here, :] = total
    spread_ref[...] = spread


def finish_kernel(weights, own, in_1, in_2, in_3, mean_ref, spread_ref):
    line = [sum(weights[4 * e + j, 0] for e in range(4)) for j in range(4)]
    total, weight = own[...], line[0]
    spread = jnp.zeros((8, 128), f32)
    for by, part in ((1, in_1), (3, in_3), (2, in_2)):
        total, more = merge_into(total, weight, part[...], line[4 - by])
        spread += more
        weight = weight + line[4 - by]
    mean_ref[...] = total / jnp.full((8, 128), weight, f32)[0:1]
    spread_ref[...] = spread


def price_kernel(slots, roster_ref, price_ref, spread_ref, weight_ref, *refs):
    means, out_ref, gap_ref = refs[:10], refs[10], refs[11]
    each = price_ref.shape[0]
    rows = means[3].shape[1]

    @pl.when(pl.program_id(0) == 0)
    def _():
        spread = jnp.sum(spread_ref[...], keepdims=True)
        gap_ref[...] = jnp.sqrt(spread / jnp.sum(weight_ref[...], keepdims=True))

    for i in range(each):
        s = pl.program_id(0) * each + i
        for side in range(2):
            slot = slots[side, s]
            first, second = slot // 4, slot % 4
            pack, one, third, two_low, two_high = means[side * 5 : side * 5 + 5]
            for k in range(4):

                @pl.when(first == k)
                def _():
                    for half in range(2):
                        if k == 2:
                            mean = (two_low, two_high)[half][second]
                        else:
                            mean = (pack, one, None, third)[k][half, second]
                        here = pl.ds((side * 2 + half) * rows, rows)
                        deviation = roster_ref[s, here, :] - mean
                        out_ref[i, here, :] = (
                            price_ref[i, here, :].astype(f32) + penalty * deviation
                        ).astype(bf16)


def veh_pairs(kind):
    if kind == "core":
        return [(i, i ^ 1) for i in range(8)]
    return [(z * 2 + c, kind[z] * 2 + c) for z in range(4) for c in range(2)]


def scen_pairs(pair, axis):
    out = []
    for y in range(4):
        for x in range(4):
            to = (y * 4 + pair[x]) if axis == "x" else (pair[y] * 4 + x)
            out.append((y * 4 + x, to))
    return out


def usage_exchange(value):
    value = value + lax.ppermute(value, "veh", veh_pairs("core"))
    turns = [
        lax.ppermute(value, "veh", veh_pairs({z: (z + by) % 4 for z in range(4)}))
        for by in (1, 3, 2)
    ]
    return [value, turns[0], turns[2], turns[1]]


def spread_over_veh(value):
    for kind in ("core", PAIR_A, PAIR_B):
        value = value + lax.ppermute(value, "veh", veh_pairs(kind))
    return value


def sum_over_scen(value):
    for axis in ("x", "y"):
        for pair in (PAIR_A, PAIR_B):
            value = value + lax.ppermute(value, "scen", scen_pairs(pair, axis))
    return value


def shift(value, axis, by):
    pairs = []
    for y in range(4):
        for x in range(4):
            to = (y * 4 + (x + by) % 4) if axis == "x" else (((y + by) % 4) * 4 + x)
            pairs.append((y * 4 + x, to))
    return lax.ppermute(value, "scen", pairs)


def vmem_spec():
    return pl.BlockSpec(memory_space=pltpu.VMEM)


def in_vmem(value):
    return pltpu.with_memory_space_constraint(value, pltpu.VMEM)


def in_hbm(value):
    return pltpu.with_memory_space_constraint(value, pltpu.HBM)


def local_call(body, weights, arrays, out_shapes, name):
    return pl.pallas_call(
        body,
        in_specs=[pl.BlockSpec(memory_space=pltpu.SMEM)] + [vmem_spec()] * len(arrays),
        out_specs=[vmem_spec()] * (len(out_shapes) + 1),
        out_shape=[pltpu.VMEM(shape, f32) for shape in out_shapes] + [pltpu.VMEM((8, 128), f32)],
        compiler_params=pltpu.CompilerParams(vmem_limit_bytes=LIMIT),
        name=name,
    )(weights, *[in_vmem(a) for a in arrays])


def gather_row(own, second):
    return {0: own, **{by: shift(own, second, -by) for by in (1, 3, 2)}}


def gather_pack(row):
    rows = row[0].shape[0] // 2
    return jnp.stack([row[k].reshape(2, rows, -1) for k in range(4)], axis=1)


def gather_near(pack, first):
    return pack, shift(pack, first, -1), shift(pack, first, 1)


def gather_far(pack, one, third, first):
    two_low = shift(third[0], first, 1)
    two_high = shift(one[1], first, -1)
    return [pack, one, third, two_low, two_high]


def shards(
    start_plan,
    linear_cost,
    price,
    anchor,
    hessian,
    usage_coef,
    crew_limit,
    crew_dual,
    crew_row,
    bundle_of,
    scen_weight,
):
    count, vehicles, n = start_plan.shape
    crews = crew_limit.shape[1]
    bundle_count = anchor.shape[0]
    me = lax.axis_index("scen")
    all_bundles = bundle_of[:, 0]
    my_bundles = lax.dynamic_slice_in_dim(all_bundles, me * count, count)
    all_weights = scen_weight.astype(f32)
    my_weights = lax.dynamic_slice_in_dim(all_weights, me * count, count)

    pad = ((0, 0), (0, CREW_PAD - crews))
    limit = jnp.pad(crew_limit, pad)
    dual = jnp.pad(crew_dual, pad)
    def per_scen(*shape):
        return pl.BlockSpec((1, *shape), lambda s, *_: (s, 0, 0))

    def whole(*shape):
        return pl.BlockSpec(shape, lambda s, *_: (0,) * len(shape))

    params = pltpu.CompilerParams(
        dimension_semantics=("arbitrary",), vmem_limit_bytes=LIMIT
    )
    tall = pltpu.VMEM((count, n, vehicles), f32)
    flat_block = per_scen(vehicles, n)
    pair_block = pl.BlockSpec((2, vehicles, n), lambda s, *_: (s, 0, 0))
    vm = vmem_spec()

    partial, linear, coef_t, row_to_veh, usage = pl.pallas_call(
        first_kernel,
        grid_spec=pltpu.PrefetchScalarGridSpec(
            num_scalar_prefetch=1,
            grid=(count // 2,),
            in_specs=[
                pair_block,
                pair_block,
                pair_block,
                pl.BlockSpec((1, vehicles, n), lambda s, b: (b[2 * s], 0, 0)),
                pl.BlockSpec((1, vehicles, n), lambda s, b: (b[2 * s + 1], 0, 0)),
                pl.BlockSpec((2, n, n), lambda s, *_: (s, 0, 0)),
                whole(vehicles, n),
                whole(count, crews),
                whole(1, vehicles),
            ],
            out_specs=[vm] * 5,
            scratch_shapes=[
                pltpu.VMEM((16, 1, vehicles), f32),
                pltpu.VMEM((56, 8, vehicles), f32),
                pltpu.VMEM((2 * n, 2 * n), bf16),
                pltpu.VMEM((count, CREW_PAD), f32),
            ],
        ),
        out_shape=[
            tall,
            tall,
            pltpu.VMEM((n, vehicles), f32),
            pltpu.VMEM((CREW_PAD, vehicles), bf16),
            pltpu.VMEM((56, CREW_PAD), f32),
        ],
        compiler_params=params,
        name="first_steps",
    )(
        my_bundles,
        in_hbm(start_plan),
        in_hbm(linear_cost),
        in_hbm(price),
        in_hbm(anchor),
        in_hbm(anchor),
        in_hbm(hessian),
        in_hbm(usage_coef),
        crew_dual,
        crew_row[None, :],
    )

    use = usage_exchange(usage)
    norms = summed(*[u[48:56] for u in use])
    for _ in range(3):
        partial, usage, dual = pl.pallas_call(
            middle_kernel,
            in_specs=[vm] * 12,
            out_specs=[vm] * 3,
            out_shape=[
                tall,
                pltpu.VMEM((48, CREW_PAD), f32),
                pltpu.VMEM((count, CREW_PAD), f32),
            ],
            input_output_aliases={0: 0},
            scratch_shapes=[
                pltpu.VMEM((48, 1, vehicles), f32),
                pltpu.VMEM((48, 8, vehicles), f32),
                pltpu.VMEM((2 * n, 2 * n), bf16),
            ],
            compiler_params=pltpu.CompilerParams(vmem_limit_bytes=LIMIT),
            name="three_steps",
        )(
            *[
                in_vmem(a)
                for a in (
                    partial,
                    linear,
                    hessian,
                    coef_t,
                    *use,
                    norms,
                    limit,
                    dual,
                    row_to_veh,
                )
            ]
        )
        use = usage_exchange(usage)

    me_y, me_x = np.arange(16)[:, None] // 4, np.arange(16)[:, None] % 4
    it_y, it_x = np.arange(16)[None, :] // 4, np.arange(16)[None, :] % 4
    place_a = ((it_x - me_x) % 4) * 4 + (it_y - me_y) % 4
    place_b = ((it_y - me_y) % 4) * 4 + (it_x - me_x) % 4
    here = jnp.arange(16, dtype=jnp.int32) == me
    row_a = jnp.sum(jnp.where(here[:, None], place_a, 0), axis=0)
    row_b = jnp.sum(jnp.where(here[:, None], place_b, 0), axis=0)
    ids = jnp.arange(16, dtype=jnp.int32)
    hot = my_bundles[:, None] == ids[None, :]
    slots = jnp.stack(
        [jnp.sum(jnp.where(hot, row[None, :], 0), axis=1) for row in (row_a, row_b)]
    ).astype(jnp.int32)
    same = my_bundles[:, None] == my_bundles[None, :]
    before = jnp.arange(count)[None, :] < jnp.arange(count)[:, None]
    held = jnp.sum(jnp.where(same & before, my_weights[None, :], 0.0), axis=1)
    factors = jnp.stack(
        [
            my_weights,
            held * my_weights / (held + my_weights),
            1.0 / jnp.maximum(held, 1.0),
        ]
    )
    half = vehicles // 2
    bundle_sums = pltpu.VMEM((bundle_count, half, n), f32)
    quarter = pltpu.VMEM((4, half // 2, n), f32)
    plan, roster, sum_a, sum_b, up_a, down_a, up_b, down_b, spread, dual = pl.pallas_call(
        last_kernel,
        grid_spec=pltpu.PrefetchScalarGridSpec(
            num_scalar_prefetch=2,
            grid=(count,),
            in_specs=[vm] * 12,
            out_specs=[flat_block] + [vm] * 9,
            scratch_shapes=[pltpu.VMEM((32, 1, vehicles), f32)],
        ),
        out_shape=[
            jax.ShapeDtypeStruct((count, vehicles, n), bf16),
            pltpu.VMEM((count, vehicles, n), f32),
            bundle_sums,
            bundle_sums,
            quarter,
            quarter,
            quarter,
            quarter,
            pltpu.VMEM((8, n), f32),
            pltpu.VMEM((count, CREW_PAD), f32),
        ],
        compiler_params=params,
        name="last_step",
    )(
        slots,
        factors,
        *[
            in_vmem(a)
            for a in (
                partial,
                linear,
                hessian,
                coef_t,
                *use,
                norms,
                limit,
                dual,
                row_to_veh,
            )
        ],
    )

    owners = jnp.arange(all_bundles.shape[0], dtype=jnp.int32) // count

    def weight_table(row):
        device = jnp.sum(jnp.where(owners[:, None] == ids[None, :], row[None, :], 0), axis=1)
        bundle = jnp.sum(jnp.where(all_bundles[:, None] == ids[None, :], row[None, :], 0), axis=1)
        return jnp.sum(
            jnp.where(
                (device[None, None, :] == ids[:, None, None])
                & (bundle[None, None, :] == ids[None, :, None]),
                all_weights[None, None, :],
                0.0,
            ),
            axis=2,
        )

    weights_a = weight_table(row_a)
    weights_b = weight_table(row_b)

    sides = (
        ("x", "y", weights_a, sum_a, up_a, down_a),
        ("y", "x", weights_b, sum_b, up_b, down_b),
    )
    flow = (2, 4, half // 2, n)
    flat = (half, n)
    moved = [(shift(up, f, 1), shift(down, f, -1)) for f, _, _, _, up, down in sides]
    moved = [
        local_call(forward_kernel, w, (sums, up, down), [flow, flow], "forward")
        for (_, _, w, sums, _, _), (up, down) in zip(sides, moved)
    ]
    spreads = [spread] + [m[2] for m in moved]
    moved = [(shift(m[0], side[0], 1), shift(m[1], side[0], -1)) for side, m in zip(sides, moved)]
    moved = [
        local_call(arrive_kernel, w, (sums, up, down), [flat] * 4, "arrive")
        for (_, _, w, sums, _, _), (up, down) in zip(sides, moved)
    ]
    spreads += [m[4] for m in moved]
    moved = [
        (m[0], *[shift(m[by], side[1], by) for by in (1, 2, 3)]) for side, m in zip(sides, moved)
    ]
    moved = [
        local_call(finish_kernel, side[2], m, [flat], "finish") for side, m in zip(sides, moved)
    ]
    spreads += [m[1] for m in moved]
    own_a, own_b = moved[0][0], moved[1][0]
    row_a, row_b = gather_row(own_a, "y"), gather_row(own_b, "x")
    pack_a, pack_b = gather_pack(row_a), gather_pack(row_b)
    pack_a, pack_b, spread = lax.optimization_barrier((pack_a, pack_b, sum(spreads)))
    near_a, near_b = gather_near(pack_a, "x"), gather_near(pack_b, "y")
    spread = spread_over_veh(spread)
    spread_total = sum_over_scen(spread)
    means = gather_far(*near_a, "x") + gather_far(*near_b, "y")
    entries = vehicles * lax.axis_size("veh") * n

    each = 2
    new_price, gap = pl.pallas_call(
        price_kernel,
        grid_spec=pltpu.PrefetchScalarGridSpec(
            num_scalar_prefetch=1,
            grid=(count // each,),
            in_specs=[vm, pair_block] + [vm] * 12,
            out_specs=[pair_block, whole(1, 1)],
        ),
        out_shape=[
            jax.ShapeDtypeStruct((count, vehicles, n), bf16),
            jax.ShapeDtypeStruct((1, 1), f32),
        ],
        compiler_params=params,
        name="new_price",
    )(
        slots,
        in_vmem(roster),
        in_hbm(price),
        in_vmem(spread_total),
        in_vmem((all_weights * entries)[None, :]),
        *[in_vmem(m) for m in means],
    )

    own_mean = jnp.concatenate([own_a, own_b], axis=0)
    return (plan, new_price, own_mean.astype(bf16)[None], dual[:, :crews], gap[0, 0])


def solution(mesh):
    return jax.shard_map(
        shards,
        mesh=mesh,
        in_specs=(
            P("scen", "veh", None),
            P("scen", "veh", None),
            P("scen", "veh", None),
            P(None, "veh", None),
            P("scen", None, None),
            P("veh", None),
            P("scen", None),
            P("scen", None),
            P("veh"),
            P(),
            P(),
        ),
        out_specs=(
            P("scen", "veh", None),
            P("scen", "veh", None),
            P("scen", "veh", None),
            P("scen", None),
            P(),
        ),
        check_vma=False,
    )
```

```python
import functools

import jax
import jax.numpy as jnp
import numpy as np
from jax import lax
from jax.experimental import pallas as pl
from jax.experimental.pallas import tpu as pltpu
from jax.sharding import PartitionSpec as P

ITERS = 12
penalty = 1.0
step_size = 0.02
dual_step = 0.02
keep = 1.0 - step_size * penalty
CREW_PAD = 384
LIMIT = 14 * 1024 * 1024
bf16 = jnp.bfloat16
f32 = jnp.float32

PAIR_A = {0: 1, 1: 0, 2: 3, 3: 2}
PAIR_B = {0: 3, 3: 0, 1: 2, 2: 1}


def split3(value):
    hi = value.astype(bf16)
    rest = value - hi.astype(f32)
    mid = rest.astype(bf16)
    low = (rest - mid.astype(f32)).astype(bf16)
    return jnp.concatenate([hi, mid, low], axis=0)


def exact_dot(left, right):
    rows = left.shape[0]
    out = jnp.dot(split3(left), right, preferred_element_type=f32)
    return out[:rows] + out[rows : 2 * rows] + out[2 * rows :]


def folded(value):
    return jnp.sum(value.reshape(-1, 8, value.shape[1]), axis=0)


def used_dot(used, row_to_veh):
    flat = jnp.sum(used, axis=1)
    rows = flat.shape[0]
    out = lax.dot_general(
        split3(flat), row_to_veh, (((1,), (1,)), ((), ())), preferred_element_type=f32
    )
    return out[:rows] + out[rows : 2 * rows] + out[2 * rows :]


def first_kernel(
    bundles,
    start_ref,
    cost_ref,
    price_ref,
    anchor_0,
    anchor_1,
    hess_ref,
    coef_ref,
    dual_ref,
    row_ref,
    partial_ref,
    linear_ref,
    coef_t_ref,
    row_to_veh,
    usage_ref,
    crew_scr,
    used_scr,
    block_scr,
    dual_scr,
):
    step = pl.program_id(0)
    count = pl.num_programs(0)
    n = hess_ref.shape[-1]

    @pl.when(step == 0)
    def _():
        block_scr[...] = jnp.zeros_like(block_scr)
        ids = lax.broadcasted_iota(jnp.int32, row_to_veh.shape, 0)
        row_to_veh[...] = (ids == row_ref[...]).astype(f32).astype(bf16)
        dual_scr[...] = jnp.zeros_like(dual_scr)
        dual_scr[:, : dual_ref.shape[1]] = dual_ref[...]
        crew_scr[:, 0, :] = step_size * exact_dot(dual_scr[...], row_to_veh[...])
        used_scr[48:56] = jnp.zeros_like(used_scr[48:56])
        c = coef_ref[...].astype(f32).T
        coef_t_ref[...] = c
        used_scr[48] = folded(c * c)

    block_scr[0:n, 0:n] = hess_ref[0]
    block_scr[n:, n:] = hess_ref[1]
    both = block_scr[...]
    c = coef_t_ref[...]
    s = 2 * step
    xs = []
    for i, anchor_ref in enumerate((anchor_0, anchor_1)):
        linear = step_size * (
            cost_ref[i].astype(f32) + price_ref[i].astype(f32) - penalty * anchor_ref[0].astype(f32)
        )
        linear_ref[s + i] = linear.T
        x = start_ref[i].T.astype(f32)
        used_scr[s + i] = folded(c * x)
        xs.append(x)
    for k in (1, 2):
        stacked = jnp.concatenate([x.astype(bf16) for x in xs], axis=0)
        curve = jnp.dot(both, stacked, preferred_element_type=f32)
        for i in range(2):
            x = (keep * xs[i] - linear_ref[s + i]) - step_size * curve[i * n : (i + 1) * n]
            if k < 2:
                x = x - crew_scr[s + i] * c
            used_scr[16 * k + s + i] = folded(c * x)
            xs[i] = x
    for i in range(2):
        partial_ref[s + i] = xs[i]

    @pl.when(step == count - 1)
    def _():
        usage_ref[...] = used_dot(used_scr[...], row_to_veh[...])


def summed(a, b, c, d):
    return (a[...] + c[...]) + (b[...] + d[...])


def crew_update(usage, norms, limit, dual):
    one = jnp.maximum(dual + dual_step * (usage[0:16] - limit), 0.0)
    third = usage[32:48] - step_size * one * norms
    two = jnp.maximum(one + dual_step * (usage[16:32] - limit), 0.0)
    three = jnp.maximum(two + dual_step * (third - limit), 0.0)
    return one, two, three


def middle_kernel(
    partial_ref,
    linear_ref,
    hess_ref,
    coef_t_ref,
    use_0,
    use_1,
    use_2,
    use_3,
    norms_ref,
    limit_ref,
    dual_ref,
    row_to_veh,
    next_ref,
    usage_ref,
    new_dual_ref,
    crew_scr,
    used_scr,
    block_scr,
):
    count = partial_ref.shape[0]
    n = hess_ref.shape[-1]
    one, two, three = crew_update(
        summed(use_0, use_1, use_2, use_3)[0:48], norms_ref[0:1], limit_ref[...], dual_ref[...]
    )
    new_dual_ref[...] = three
    crew_scr[:, 0, :] = step_size * exact_dot(
        jnp.concatenate([one, two, three], axis=0), row_to_veh[...]
    )
    block_scr[...] = jnp.zeros_like(block_scr)

    def two_scenarios(pair, carry):
        s = 2 * pair
        block_scr[0:n, 0:n] = hess_ref[s]
        block_scr[n:, n:] = hess_ref[s + 1]
        both = block_scr[...]
        c = coef_t_ref[...]
        xs = [partial_ref[s + i] - crew_scr[s + i] * c for i in range(2)]
        for k in (1, 2, 3):
            stacked = jnp.concatenate([x.astype(bf16) for x in xs], axis=0)
            curve = jnp.dot(both, stacked, preferred_element_type=f32)
            for i in range(2):
                x = (keep * xs[i] - linear_ref[s + i]) - step_size * curve[i * n : (i + 1) * n]
                if k < 3:
                    x = x - crew_scr[16 * k + s + i] * c
                used_scr[16 * (k - 1) + s + i] = folded(c * x)
                xs[i] = x
        for i in range(2):
            next_ref[s + i] = xs[i]
        return carry

    lax.fori_loop(0, count // 2, two_scenarios, 0)
    usage_ref[...] = used_dot(used_scr[...], row_to_veh[...])


def last_kernel(
    slots,
    factors,
    partial_ref,
    linear_ref,
    hess_ref,
    coef_t_ref,
    use_0,
    use_1,
    use_2,
    use_3,
    norms_ref,
    limit_ref,
    dual_ref,
    row_to_veh,
    plan_ref,
    roster_ref,
    sum_a,
    sum_b,
    send_au,
    send_ad,
    send_bu,
    send_bd,
    spread_ref,
    new_dual_ref,
    crew_scr,
):
    s = pl.program_id(0)
    count = pl.num_programs(0)
    rows = sum_a.shape[1]

    @pl.when(s == 0)
    def _():
        one, two, three = crew_update(
            summed(use_0, use_1, use_2, use_3)[0:48], norms_ref[0:1], limit_ref[...], dual_ref[...]
        )
        new_dual_ref[...] = three
        crew_scr[:, 0, :] = step_size * exact_dot(
            jnp.concatenate([one, two], axis=0), row_to_veh[...]
        )
        sum_a[...] = jnp.zeros_like(sum_a)
        sum_b[...] = jnp.zeros_like(sum_b)
        spread_ref[...] = jnp.zeros_like(spread_ref)

    c = coef_t_ref[...]
    x = partial_ref[s] - crew_scr[s] * c
    curve = jnp.dot(hess_ref[s], x.astype(bf16), preferred_element_type=f32)
    x = (keep * x - linear_ref[s]) - step_size * curve - crew_scr[16 + s] * c
    roster_ref[s] = x.T

    weight, merge, inverse = factors[0, s], factors[1, s], factors[2, s]
    part = 112
    spread = jnp.zeros((8, 128), f32)
    for side, sums in enumerate((sum_a, sum_b)):
        slot = slots[side, s]
        for start in range(0, rows, part):
            here = pl.ds(side * rows + start, part)
            x = roster_ref[s, here, :]
            plan_ref[0, here, :] = x.astype(bf16)
            held = sums[slot, start : start + part, :]
            gap = held * inverse - x
            spread = spread + merge * folded(gap * gap)
            sums[slot, start : start + part, :] = held + weight * x
    spread_ref[...] += spread

    @pl.when(s == count - 1)
    def _():
        for sums, up, down in ((sum_a, send_au, send_ad), (sum_b, send_bu, send_bd)):
            for k in range(4):
                up[k] = sums[8 + k, : rows // 2, :]
                down[k] = sums[8 + k, rows // 2 :, :]


def merge_into(total, weight, other, other_weight):
    weight = jnp.full((8, 128), weight, f32)
    other_weight = jnp.full((8, 128), other_weight, f32)
    both = weight + other_weight
    factor = jnp.where(both > 0, weight * other_weight / jnp.maximum(both, 1.0), 0.0)
    shape = total.shape
    total8, other8 = total.reshape(-1, 8, 128), other.reshape(-1, 8, 128)
    gap = total8 * (1.0 / jnp.maximum(weight, 1.0)) - other8 * (1.0 / jnp.maximum(other_weight, 1.0))
    return total + other, factor * jnp.sum(gap * gap, axis=0)


def forward_kernel(weights, sums, up_in, down_in, up_out, down_out, spread_ref):
    rows = sums.shape[1] // 2
    spread = jnp.zeros((8, 128), f32)
    for k in range(4):
        total, more = merge_into(sums[4 + k, :rows, :], weights[0, 4 + k], up_in[k], weights[12, 4 + k])
        spread += more
        up_out[0, k] = total
        up_out[1, k] = sums[4 + k, rows:, :]
        down_out[0, k] = sums[12 + k, :rows, :]
        total, more = merge_into(
            sums[12 + k, rows:, :], weights[0, 12 + k], down_in[k], weights[4, 12 + k]
        )
        spread += more
        down_out[1, k] = total
    spread_ref[...] = spread


def arrive_kernel(weights, sums, up_in, down_in, own, out_1, out_2, out_3, spread_ref):
    rows = sums.shape[1] // 2
    spread = jnp.zeros((8, 128), f32)
    for k, out in enumerate((own, out_1, out_2, out_3)):
        w0, w1, w2, w3 = (weights[4 * e, k] for e in range(4))
        for half in range(2):
            here = slice(half * rows, (half + 1) * rows)
            w_up, w_down = (w3 + w2, w1) if half == 0 else (w3, w1 + w2)
            total, more = merge_into(sums[k, here, :], w0, up_in[half, k], w_up)
            spread += more
            total, more = merge_into(total, w0 + w_up, down_in[half, k], w_down)
            spread += more
            out[here, :] = total
    spread_ref[...] = spread


def finish_kernel(weights, own, in_1, in_2, in_3, mean_ref, spread_ref):
    line = [sum(weights[4 * e + j, 0] for e in range(4)) for j in range(4)]
    total, weight = own[...], line[0]
    spread = jnp.zeros((8, 128), f32)
    for by, part in ((1, in_1), (3, in_3), (2, in_2)):
        total, more = merge_into(total, weight, part[...], line[4 - by])
        spread += more
        weight = weight + line[4 - by]
    mean_ref[: own.shape[0], :] = total / jnp.full((8, 128), weight, f32)[0:1]
    spread_ref[...] = spread


def finish_last_kernel(weights, own, in_1, in_2, in_3, *refs):
    others, mean_ref, spread_ref = refs[:-2], refs[-2], refs[-1]
    finish_kernel(weights, own, in_1, in_2, in_3, mean_ref, spread_ref)
    mean_ref[own.shape[0] :, :] = sum((other[...] for other in others), spread_ref[...])


def price_kernel(slots, roster_ref, price_ref, spread_ref, weight_ref, *refs):
    means, out_ref, gap_ref = refs[:10], refs[10], refs[11]
    each = price_ref.shape[0]
    rows = means[3].shape[1]

    @pl.when(pl.program_id(0) == 0)
    def _():
        spread = jnp.sum(spread_ref[...], keepdims=True)
        gap_ref[...] = jnp.sqrt(spread / jnp.sum(weight_ref[...], keepdims=True))

    for i in range(each):
        s = pl.program_id(0) * each + i
        for side in range(2):
            slot = slots[side, s]
            first, second = slot // 4, slot % 4
            pack, one, third, two_low, two_high = means[side * 5 : side * 5 + 5]
            for k in range(4):

                @pl.when(first == k)
                def _():
                    for half in range(2):
                        if k == 2:
                            mean = (two_low, two_high)[half][second]
                        else:
                            mean = (pack, one, None, third)[k][half, second]
                        here = pl.ds((side * 2 + half) * rows, rows)
                        deviation = roster_ref[s, here, :] - mean
                        out_ref[i, here, :] = (
                            price_ref[i, here, :].astype(f32) + penalty * deviation
                        ).astype(bf16)


def veh_pairs(kind):
    if kind == "core":
        return [(i, i ^ 1) for i in range(8)]
    return [(z * 2 + c, kind[z] * 2 + c) for z in range(4) for c in range(2)]


def scen_pairs(pair, axis):
    out = []
    for y in range(4):
        for x in range(4):
            to = (y * 4 + pair[x]) if axis == "x" else (pair[y] * 4 + x)
            out.append((y * 4 + x, to))
    return out


def usage_exchange(value):
    value = value + lax.ppermute(value, "veh", veh_pairs("core"))
    turns = [
        lax.ppermute(value, "veh", veh_pairs({z: (z + by) % 4 for z in range(4)}))
        for by in (1, 3, 2)
    ]
    return [value, turns[0], turns[2], turns[1]]


def spread_over_veh(value):
    for kind in ("core", PAIR_A, PAIR_B):
        value = value + lax.ppermute(value, "veh", veh_pairs(kind))
    return value


def spread_over_x(value):
    for pair in (PAIR_A, PAIR_B):
        value = value + lax.ppermute(value, "scen", scen_pairs(pair, "x"))
    return value


def shift(value, axis, by):
    pairs = []
    for y in range(4):
        for x in range(4):
            to = (y * 4 + (x + by) % 4) if axis == "x" else (((y + by) % 4) * 4 + x)
            pairs.append((y * 4 + x, to))
    return lax.ppermute(value, "scen", pairs)


def vmem_spec():
    return pl.BlockSpec(memory_space=pltpu.VMEM)


def in_vmem(value):
    return pltpu.with_memory_space_constraint(value, pltpu.VMEM)


def in_hbm(value):
    return pltpu.with_memory_space_constraint(value, pltpu.HBM)


def local_call(body, weights, arrays, out_shapes, name):
    return pl.pallas_call(
        body,
        in_specs=[pl.BlockSpec(memory_space=pltpu.SMEM)] + [vmem_spec()] * len(arrays),
        out_specs=[vmem_spec()] * (len(out_shapes) + 1),
        out_shape=[pltpu.VMEM(shape, f32) for shape in out_shapes] + [pltpu.VMEM((8, 128), f32)],
        compiler_params=pltpu.CompilerParams(vmem_limit_bytes=LIMIT),
        name=name,
    )(weights, *[in_vmem(a) for a in arrays])


def gather_row(own, second):
    return {0: own, **{by: shift(own, second, -by) for by in (1, 3, 2)}}


def gather_pack(row):
    rows = row[0].shape[0] // 2
    return jnp.stack([row[k].reshape(2, rows, -1) for k in range(4)], axis=1)


def gather_near(pack, first):
    return pack, shift(pack, first, -1), shift(pack, first, 1)


def gather_far(pack, one, third, first):
    two_low = shift(third[0], first, 1)
    two_high = shift(one[1], first, -1)
    return [pack, one, third, two_low, two_high]


def shards(
    start_plan,
    linear_cost,
    price,
    anchor,
    hessian,
    usage_coef,
    crew_limit,
    crew_dual,
    crew_row,
    bundle_of,
    scen_weight,
):
    count, vehicles, n = start_plan.shape
    crews = crew_limit.shape[1]
    bundle_count = anchor.shape[0]
    me = lax.axis_index("scen")
    all_bundles = bundle_of[:, 0]
    my_bundles = lax.dynamic_slice_in_dim(all_bundles, me * count, count)
    all_weights = scen_weight.astype(f32)
    my_weights = lax.dynamic_slice_in_dim(all_weights, me * count, count)

    pad = ((0, 0), (0, CREW_PAD - crews))
    limit = jnp.pad(crew_limit, pad)
    dual = jnp.pad(crew_dual, pad)
    def per_scen(*shape):
        return pl.BlockSpec((1, *shape), lambda s, *_: (s, 0, 0))

    def whole(*shape):
        return pl.BlockSpec(shape, lambda s, *_: (0,) * len(shape))

    params = pltpu.CompilerParams(
        dimension_semantics=("arbitrary",), vmem_limit_bytes=LIMIT
    )
    tall = pltpu.VMEM((count, n, vehicles), f32)
    flat_block = per_scen(vehicles, n)
    pair_block = pl.BlockSpec((2, vehicles, n), lambda s, *_: (s, 0, 0))
    vm = vmem_spec()

    partial, linear, coef_t, row_to_veh, usage = pl.pallas_call(
        first_kernel,
        grid_spec=pltpu.PrefetchScalarGridSpec(
            num_scalar_prefetch=1,
            grid=(count // 2,),
            in_specs=[
                pair_block,
                pair_block,
                pair_block,
                pl.BlockSpec((1, vehicles, n), lambda s, b: (b[2 * s], 0, 0)),
                pl.BlockSpec((1, vehicles, n), lambda s, b: (b[2 * s + 1], 0, 0)),
                pl.BlockSpec((2, n, n), lambda s, *_: (s, 0, 0)),
                whole(vehicles, n),
                whole(count, crews),
                whole(1, vehicles),
            ],
            out_specs=[vm] * 5,
            scratch_shapes=[
                pltpu.VMEM((16, 1, vehicles), f32),
                pltpu.VMEM((56, 8, vehicles), f32),
                pltpu.VMEM((2 * n, 2 * n), bf16),
                pltpu.VMEM((count, CREW_PAD), f32),
            ],
        ),
        out_shape=[
            tall,
            tall,
            pltpu.VMEM((n, vehicles), f32),
            pltpu.VMEM((CREW_PAD, vehicles), bf16),
            pltpu.VMEM((56, CREW_PAD), f32),
        ],
        compiler_params=params,
        name="first_steps",
    )(
        my_bundles,
        in_hbm(start_plan),
        in_hbm(linear_cost),
        in_hbm(price),
        in_hbm(anchor),
        in_hbm(anchor),
        in_hbm(hessian),
        in_hbm(usage_coef),
        crew_dual,
        crew_row[None, :],
    )

    use = usage_exchange(usage)
    norms = summed(*[u[48:56] for u in use])
    for _ in range(3):
        partial, usage, dual = pl.pallas_call(
            middle_kernel,
            in_specs=[vm] * 12,
            out_specs=[vm] * 3,
            out_shape=[
                tall,
                pltpu.VMEM((48, CREW_PAD), f32),
                pltpu.VMEM((count, CREW_PAD), f32),
            ],
            input_output_aliases={0: 0},
            scratch_shapes=[
                pltpu.VMEM((48, 1, vehicles), f32),
                pltpu.VMEM((48, 8, vehicles), f32),
                pltpu.VMEM((2 * n, 2 * n), bf16),
            ],
            compiler_params=pltpu.CompilerParams(vmem_limit_bytes=LIMIT),
            name="three_steps",
        )(
            *[
                in_vmem(a)
                for a in (
                    partial,
                    linear,
                    hessian,
                    coef_t,
                    *use,
                    norms,
                    limit,
                    dual,
                    row_to_veh,
                )
            ]
        )
        use = usage_exchange(usage)

    me_y, me_x = np.arange(16)[:, None] // 4, np.arange(16)[:, None] % 4
    it_y, it_x = np.arange(16)[None, :] // 4, np.arange(16)[None, :] % 4
    place_a = ((it_x - me_x) % 4) * 4 + (it_y - me_y) % 4
    place_b = ((it_y - me_y) % 4) * 4 + (it_x - me_x) % 4
    here = jnp.arange(16, dtype=jnp.int32) == me
    row_a = jnp.sum(jnp.where(here[:, None], place_a, 0), axis=0)
    row_b = jnp.sum(jnp.where(here[:, None], place_b, 0), axis=0)
    ids = jnp.arange(16, dtype=jnp.int32)
    hot = my_bundles[:, None] == ids[None, :]
    slots = jnp.stack(
        [jnp.sum(jnp.where(hot, row[None, :], 0), axis=1) for row in (row_a, row_b)]
    ).astype(jnp.int32)
    same = my_bundles[:, None] == my_bundles[None, :]
    before = jnp.arange(count)[None, :] < jnp.arange(count)[:, None]
    held = jnp.sum(jnp.where(same & before, my_weights[None, :], 0.0), axis=1)
    factors = jnp.stack(
        [
            my_weights,
            held * my_weights / (held + my_weights),
            1.0 / jnp.maximum(held, 1.0),
        ]
    )
    half = vehicles // 2
    bundle_sums = pltpu.VMEM((bundle_count, half, n), f32)
    quarter = pltpu.VMEM((4, half // 2, n), f32)
    plan, roster, sum_a, sum_b, up_a, down_a, up_b, down_b, spread, dual = pl.pallas_call(
        last_kernel,
        grid_spec=pltpu.PrefetchScalarGridSpec(
            num_scalar_prefetch=2,
            grid=(count,),
            in_specs=[vm] * 12,
            out_specs=[flat_block] + [vm] * 9,
            scratch_shapes=[pltpu.VMEM((32, 1, vehicles), f32)],
        ),
        out_shape=[
            jax.ShapeDtypeStruct((count, vehicles, n), bf16),
            pltpu.VMEM((count, vehicles, n), f32),
            bundle_sums,
            bundle_sums,
            quarter,
            quarter,
            quarter,
            quarter,
            pltpu.VMEM((8, n), f32),
            pltpu.VMEM((count, CREW_PAD), f32),
        ],
        compiler_params=params,
        name="last_step",
    )(
        slots,
        factors,
        *[
            in_vmem(a)
            for a in (
                partial,
                linear,
                hessian,
                coef_t,
                *use,
                norms,
                limit,
                dual,
                row_to_veh,
            )
        ],
    )

    owners = jnp.arange(all_bundles.shape[0], dtype=jnp.int32) // count

    def weight_table(row):
        device = jnp.sum(jnp.where(owners[:, None] == ids[None, :], row[None, :], 0), axis=1)
        bundle = jnp.sum(jnp.where(all_bundles[:, None] == ids[None, :], row[None, :], 0), axis=1)
        return jnp.sum(
            jnp.where(
                (device[None, None, :] == ids[:, None, None])
                & (bundle[None, None, :] == ids[None, :, None]),
                all_weights[None, None, :],
                0.0,
            ),
            axis=2,
        )

    weights_a = weight_table(row_a)
    weights_b = weight_table(row_b)

    sides = (
        ("x", "y", weights_a, sum_a, up_a, down_a),
        ("y", "x", weights_b, sum_b, up_b, down_b),
    )
    flow = (2, 4, half // 2, n)
    flat = (half, n)
    moved = [(shift(up, f, 1), shift(down, f, -1)) for f, _, _, _, up, down in sides]
    moved = [
        local_call(forward_kernel, w, (sums, up, down), [flow, flow], "forward")
        for (_, _, w, sums, _, _), (up, down) in zip(sides, moved)
    ]
    spreads = [spread] + [m[2] for m in moved]
    moved = [(shift(m[0], side[0], 1), shift(m[1], side[0], -1)) for side, m in zip(sides, moved)]
    moved = [
        local_call(arrive_kernel, w, (sums, up, down), [flat] * 4, "arrive")
        for (_, _, w, sums, _, _), (up, down) in zip(sides, moved)
    ]
    spreads += [m[4] for m in moved]
    moved = [
        (m[0], *[shift(m[by], side[1], by) for by in (1, 2, 3)]) for side, m in zip(sides, moved)
    ]
    own_b, spread = local_call(finish_kernel, sides[1][2], moved[1], [flat], "finish")
    own_a = local_call(
        finish_last_kernel, sides[0][2], (*moved[0], *spreads, spread), [(half + 8, n)], "finish"
    )[0]
    row_a, row_b = gather_row(own_a, "y"), gather_row(own_b, "x")
    spread = summed(*[row_a[k][half:] for k in range(4)])
    row_a = {k: row_a[k][:half] for k in range(4)}
    pack_a, pack_b = gather_pack(row_a), gather_pack(row_b)
    pack_a, pack_b, spread = lax.optimization_barrier((pack_a, pack_b, spread))
    near_a, near_b = gather_near(pack_a, "x"), gather_near(pack_b, "y")
    spread = spread_over_veh(spread)
    spread_total = spread_over_x(spread)
    means = gather_far(*near_a, "x") + gather_far(*near_b, "y")
    entries = vehicles * lax.axis_size("veh") * n

    each = 2
    new_price, gap = pl.pallas_call(
        price_kernel,
        grid_spec=pltpu.PrefetchScalarGridSpec(
            num_scalar_prefetch=1,
            grid=(count // each,),
            in_specs=[vm, pair_block] + [vm] * 12,
            out_specs=[pair_block, whole(1, 1)],
        ),
        out_shape=[
            jax.ShapeDtypeStruct((count, vehicles, n), bf16),
            jax.ShapeDtypeStruct((1, 1), f32),
        ],
        compiler_params=params,
        name="new_price",
    )(
        slots,
        in_vmem(roster),
        in_hbm(price),
        in_vmem(spread_total),
        in_vmem((all_weights * entries)[None, :]),
        *[in_vmem(m) for m in means],
    )

    own_mean = jnp.concatenate([own_a[:half], own_b], axis=0)
    return (plan, new_price, own_mean.astype(bf16)[None], dual[:, :crews], gap[0, 0])


def solution(mesh):
    return jax.shard_map(
        shards,
        mesh=mesh,
        in_specs=(
            P("scen", "veh", None),
            P("scen", "veh", None),
            P("scen", "veh", None),
            P(None, "veh", None),
            P("scen", None, None),
            P("veh", None),
            P("scen", None),
            P("scen", None),
            P("veh"),
            P(),
            P(),
        ),
        out_specs=(
            P("scen", "veh", None),
            P("scen", "veh", None),
            P("scen", "veh", None),
            P("scen", None),
            P(),
        ),
        check_vma=False,
    )
```

```python
import functools

import jax
import jax.numpy as jnp
import numpy as np
from jax import lax
from jax.experimental import pallas as pl
from jax.experimental.pallas import tpu as pltpu
from jax.sharding import PartitionSpec as P

ITERS = 12
penalty = 1.0
step_size = 0.02
dual_step = 0.02
keep = 1.0 - step_size * penalty
CREW_PAD = 384
LIMIT = 14 * 1024 * 1024
bf16 = jnp.bfloat16
f32 = jnp.float32

PAIR_A = {0: 1, 1: 0, 2: 3, 3: 2}
PAIR_B = {0: 3, 3: 0, 1: 2, 2: 1}


def split3(value):
    hi = value.astype(bf16)
    rest = value - hi.astype(f32)
    mid = rest.astype(bf16)
    low = (rest - mid.astype(f32)).astype(bf16)
    return jnp.concatenate([hi, mid, low], axis=0)


def exact_dot(left, right):
    rows = left.shape[0]
    out = jnp.dot(split3(left), right, preferred_element_type=f32)
    return out[:rows] + out[rows : 2 * rows] + out[2 * rows :]


def folded(value):
    return jnp.sum(value.reshape(-1, 8, value.shape[1]), axis=0)


def used_dot(used, row_to_veh):
    flat = jnp.sum(used, axis=1)
    rows = flat.shape[0]
    out = lax.dot_general(
        split3(flat), row_to_veh, (((1,), (1,)), ((), ())), preferred_element_type=f32
    )
    return out[:rows] + out[rows : 2 * rows] + out[2 * rows :]


def first_kernel(
    bundles,
    start_ref,
    cost_ref,
    price_ref,
    anchor_0,
    anchor_1,
    hess_ref,
    coef_ref,
    dual_ref,
    row_ref,
    partial_ref,
    linear_ref,
    coef_t_ref,
    row_to_veh,
    usage_ref,
    crew_scr,
    used_scr,
    block_scr,
    dual_scr,
):
    step = pl.program_id(0)
    count = pl.num_programs(0)
    n = hess_ref.shape[-1]

    @pl.when(step == 0)
    def _():
        block_scr[...] = jnp.zeros_like(block_scr)
        ids = lax.broadcasted_iota(jnp.int32, row_to_veh.shape, 0)
        row_to_veh[...] = (ids == row_ref[...]).astype(f32).astype(bf16)
        dual_scr[...] = jnp.zeros_like(dual_scr)
        dual_scr[:, : dual_ref.shape[1]] = dual_ref[...]
        crew_scr[:, 0, :] = step_size * exact_dot(dual_scr[...], row_to_veh[...])
        used_scr[48:56] = jnp.zeros_like(used_scr[48:56])
        c = coef_ref[...].astype(f32).T
        coef_t_ref[...] = c
        used_scr[48] = folded(c * c)

    block_scr[0:n, 0:n] = hess_ref[0]
    block_scr[n:, n:] = hess_ref[1]
    both = block_scr[...]
    c = coef_t_ref[...]
    s = 2 * step
    xs = []
    for i, anchor_ref in enumerate((anchor_0, anchor_1)):
        linear = step_size * (
            cost_ref[i].astype(f32) + price_ref[i].astype(f32) - penalty * anchor_ref[0].astype(f32)
        )
        linear_ref[s + i] = linear.T
        x = start_ref[i].T.astype(f32)
        used_scr[s + i] = folded(c * x)
        xs.append(x)
    for k in (1, 2):
        stacked = jnp.concatenate([x.astype(bf16) for x in xs], axis=0)
        curve = jnp.dot(both, stacked, preferred_element_type=f32)
        for i in range(2):
            x = (keep * xs[i] - linear_ref[s + i]) - step_size * curve[i * n : (i + 1) * n]
            if k < 2:
                x = x - crew_scr[s + i] * c
            used_scr[16 * k + s + i] = folded(c * x)
            xs[i] = x
    for i in range(2):
        partial_ref[s + i] = xs[i]

    @pl.when(step == count - 1)
    def _():
        usage_ref[...] = used_dot(used_scr[...], row_to_veh[...])


def summed(a, b, c, d):
    return (a[...] + c[...]) + (b[...] + d[...])


def crew_update(usage, norms, limit, dual):
    one = jnp.maximum(dual + dual_step * (usage[0:16] - limit), 0.0)
    third = usage[32:48] - step_size * one * norms
    two = jnp.maximum(one + dual_step * (usage[16:32] - limit), 0.0)
    three = jnp.maximum(two + dual_step * (third - limit), 0.0)
    return one, two, three


def middle_kernel(
    partial_ref,
    linear_ref,
    hess_ref,
    coef_t_ref,
    use_0,
    use_1,
    use_2,
    use_3,
    norms_ref,
    limit_ref,
    dual_ref,
    row_to_veh,
    next_ref,
    usage_ref,
    new_dual_ref,
    crew_scr,
    used_scr,
    block_scr,
):
    count = partial_ref.shape[0]
    n = hess_ref.shape[-1]
    one, two, three = crew_update(
        summed(use_0, use_1, use_2, use_3)[0:48], norms_ref[0:1], limit_ref[...], dual_ref[...]
    )
    new_dual_ref[...] = three
    crew_scr[:, 0, :] = step_size * exact_dot(
        jnp.concatenate([one, two, three], axis=0), row_to_veh[...]
    )
    block_scr[...] = jnp.zeros_like(block_scr)

    def two_scenarios(pair, carry):
        s = 2 * pair
        block_scr[0:n, 0:n] = hess_ref[s]
        block_scr[n:, n:] = hess_ref[s + 1]
        both = block_scr[...]
        c = coef_t_ref[...]
        xs = [partial_ref[s + i] - crew_scr[s + i] * c for i in range(2)]
        for k in (1, 2, 3):
            stacked = jnp.concatenate([x.astype(bf16) for x in xs], axis=0)
            curve = jnp.dot(both, stacked, preferred_element_type=f32)
            for i in range(2):
                x = (keep * xs[i] - linear_ref[s + i]) - step_size * curve[i * n : (i + 1) * n]
                if k < 3:
                    x = x - crew_scr[16 * k + s + i] * c
                used_scr[16 * (k - 1) + s + i] = folded(c * x)
                xs[i] = x
        for i in range(2):
            next_ref[s + i] = xs[i]
        return carry

    lax.fori_loop(0, count // 2, two_scenarios, 0)
    usage_ref[...] = used_dot(used_scr[...], row_to_veh[...])


def last_kernel(
    slots,
    factors,
    partial_ref,
    linear_ref,
    hess_ref,
    coef_t_ref,
    use_0,
    use_1,
    use_2,
    use_3,
    norms_ref,
    limit_ref,
    dual_ref,
    row_to_veh,
    plan_ref,
    roster_ref,
    sum_a,
    sum_b,
    send_au,
    send_ad,
    send_bu,
    send_bd,
    spread_ref,
    new_dual_ref,
    crew_scr,
):
    s = pl.program_id(0)
    count = pl.num_programs(0)
    rows = sum_a.shape[1]

    @pl.when(s == 0)
    def _():
        one, two, three = crew_update(
            summed(use_0, use_1, use_2, use_3)[0:48], norms_ref[0:1], limit_ref[...], dual_ref[...]
        )
        new_dual_ref[...] = three
        crew_scr[:, 0, :] = step_size * exact_dot(
            jnp.concatenate([one, two], axis=0), row_to_veh[...]
        )
        sum_a[...] = jnp.zeros_like(sum_a)
        sum_b[...] = jnp.zeros_like(sum_b)
        spread_ref[...] = jnp.zeros_like(spread_ref)

    c = coef_t_ref[...]
    x = partial_ref[s] - crew_scr[s] * c
    curve = jnp.dot(hess_ref[s], x.astype(bf16), preferred_element_type=f32)
    x = (keep * x - linear_ref[s]) - step_size * curve - crew_scr[16 + s] * c
    roster_ref[s] = x.T

    weight, merge, inverse = factors[0, s], factors[1, s], factors[2, s]
    part = 112
    spread = jnp.zeros((8, 128), f32)
    for side, sums in enumerate((sum_a, sum_b)):
        slot = slots[side, s]
        for start in range(0, rows, part):
            here = pl.ds(side * rows + start, part)
            x = roster_ref[s, here, :]
            plan_ref[0, here, :] = x.astype(bf16)
            held = sums[slot, start : start + part, :]
            gap = held * inverse - x
            spread = spread + merge * folded(gap * gap)
            sums[slot, start : start + part, :] = held + weight * x
    spread_ref[...] += spread

    @pl.when(s == count - 1)
    def _():
        for sums, up, down in ((sum_a, send_au, send_ad), (sum_b, send_bu, send_bd)):
            for k in range(4):
                up[k] = sums[8 + k, : rows // 2, :]
                down[k] = sums[8 + k, rows // 2 :, :]


def merge_into(total, weight, other, other_weight):
    weight = jnp.full((8, 128), weight, f32)
    other_weight = jnp.full((8, 128), other_weight, f32)
    both = weight + other_weight
    factor = jnp.where(both > 0, weight * other_weight / jnp.maximum(both, 1.0), 0.0)
    shape = total.shape
    total8, other8 = total.reshape(-1, 8, 128), other.reshape(-1, 8, 128)
    gap = total8 * (1.0 / jnp.maximum(weight, 1.0)) - other8 * (1.0 / jnp.maximum(other_weight, 1.0))
    return total + other, factor * jnp.sum(gap * gap, axis=0)


def forward_kernel(weights, sums, up_in, down_in, up_out, down_out, spread_ref):
    rows = sums.shape[1] // 2
    spread = jnp.zeros((8, 128), f32)
    for k in range(4):
        total, more = merge_into(sums[4 + k, :rows, :], weights[0, 4 + k], up_in[k], weights[12, 4 + k])
        spread += more
        up_out[0, k] = total
        up_out[1, k] = sums[4 + k, rows:, :]
        down_out[0, k] = sums[12 + k, :rows, :]
        total, more = merge_into(
            sums[12 + k, rows:, :], weights[0, 12 + k], down_in[k], weights[4, 12 + k]
        )
        spread += more
        down_out[1, k] = total
    spread_ref[...] = spread


def arrive_kernel(weights, sums, up_in, down_in, own, out_1, out_2, out_3, spread_ref):
    rows = sums.shape[1] // 2
    spread = jnp.zeros((8, 128), f32)
    for k, out in enumerate((own, out_1, out_2, out_3)):
        w0, w1, w2, w3 = (weights[4 * e, k] for e in range(4))
        for half in range(2):
            here = slice(half * rows, (half + 1) * rows)
            w_up, w_down = (w3 + w2, w1) if half == 0 else (w3, w1 + w2)
            total, more = merge_into(sums[k, here, :], w0, up_in[half, k], w_up)
            spread += more
            total, more = merge_into(total, w0 + w_up, down_in[half, k], w_down)
            spread += more
            out[here, :] = total
    spread_ref[...] = spread


def finish_kernel(weights, own, in_1, in_2, in_3, mean_ref, spread_ref):
    line = [sum(weights[4 * e + j, 0] for e in range(4)) for j in range(4)]
    total, weight = own[...], line[0]
    spread = jnp.zeros((8, 128), f32)
    for by, part in ((1, in_1), (3, in_3), (2, in_2)):
        total, more = merge_into(total, weight, part[...], line[4 - by])
        spread += more
        weight = weight + line[4 - by]
    mean_ref[: own.shape[0], :] = total / jnp.full((8, 128), weight, f32)[0:1]
    spread_ref[...] = spread


def finish_last_kernel(weights, own, in_1, in_2, in_3, *refs):
    others, mean_ref, spread_ref = refs[:-2], refs[-2], refs[-1]
    finish_kernel(weights, own, in_1, in_2, in_3, mean_ref, spread_ref)
    mean_ref[own.shape[0] :, :] = sum((other[...] for other in others), spread_ref[...])


def price_kernel(slots, roster_ref, price_ref, spread_ref, weight_ref, *refs):
    means, out_ref, gap_ref = refs[:10], refs[10], refs[11]
    each = price_ref.shape[0]
    rows = means[3].shape[1]

    @pl.when(pl.program_id(0) == 0)
    def _():
        spread = jnp.sum(spread_ref[...], keepdims=True)
        gap_ref[...] = jnp.sqrt(spread / jnp.sum(weight_ref[...], keepdims=True))

    for i in range(each):
        s = pl.program_id(0) * each + i
        for side in range(2):
            slot = slots[side, s]
            first, second = slot // 4, slot % 4
            pack, one, third, two_low, two_high = means[side * 5 : side * 5 + 5]
            for k in range(4):

                @pl.when(first == k)
                def _():
                    for half in range(2):
                        if k == 2:
                            mean = (two_low, two_high)[half][second]
                        else:
                            mean = (pack, one, None, third)[k][half, second]
                        here = pl.ds((side * 2 + half) * rows, rows)
                        deviation = roster_ref[s, here, :] - mean
                        out_ref[i, here, :] = (
                            price_ref[i, here, :].astype(f32) + penalty * deviation
                        ).astype(bf16)


def veh_pairs(kind):
    if kind == "core":
        return [(i, i ^ 1) for i in range(8)]
    return [(z * 2 + c, kind[z] * 2 + c) for z in range(4) for c in range(2)]


def scen_pairs(pair, axis):
    out = []
    for y in range(4):
        for x in range(4):
            to = (y * 4 + pair[x]) if axis == "x" else (pair[y] * 4 + x)
            out.append((y * 4 + x, to))
    return out


def usage_exchange(value):
    value = value + lax.ppermute(value, "veh", veh_pairs("core"))
    turns = [
        lax.ppermute(value, "veh", veh_pairs({z: (z + by) % 4 for z in range(4)}))
        for by in (1, 3, 2)
    ]
    return [value, turns[0], turns[2], turns[1]]


def spread_over_veh(value):
    for kind in ("core", PAIR_A, PAIR_B):
        value = value + lax.ppermute(value, "veh", veh_pairs(kind))
    return value


def spread_over_x(value):
    for pair in (PAIR_A, PAIR_B):
        value = value + lax.ppermute(value, "scen", scen_pairs(pair, "x"))
    return value


def shift(value, axis, by):
    pairs = []
    for y in range(4):
        for x in range(4):
            to = (y * 4 + (x + by) % 4) if axis == "x" else (((y + by) % 4) * 4 + x)
            pairs.append((y * 4 + x, to))
    return lax.ppermute(value, "scen", pairs)


def vmem_spec():
    return pl.BlockSpec(memory_space=pltpu.VMEM)


def in_vmem(value):
    return pltpu.with_memory_space_constraint(value, pltpu.VMEM)


def in_hbm(value):
    return pltpu.with_memory_space_constraint(value, pltpu.HBM)


def local_call(body, weights, arrays, out_shapes, name):
    return pl.pallas_call(
        body,
        in_specs=[pl.BlockSpec(memory_space=pltpu.SMEM)] + [vmem_spec()] * len(arrays),
        out_specs=[vmem_spec()] * (len(out_shapes) + 1),
        out_shape=[pltpu.VMEM(shape, f32) for shape in out_shapes] + [pltpu.VMEM((8, 128), f32)],
        compiler_params=pltpu.CompilerParams(vmem_limit_bytes=LIMIT),
        name=name,
    )(weights, *[in_vmem(a) for a in arrays])


def gather_row(own, second):
    return {0: own, **{by: shift(own, second, -by) for by in (1, 3, 2)}}


def gather_pack(row):
    rows = row[0].shape[0] // 2
    return jnp.stack([row[k].reshape(2, rows, -1) for k in range(4)], axis=1)


def gather_near(pack, first):
    return pack, shift(pack, first, -1), shift(pack, first, 1)


def gather_far(pack, one, third, first):
    two_low = shift(third[0], first, 1)
    two_high = shift(one[1], first, -1)
    return [pack, one, third, two_low, two_high]


def shards(
    start_plan,
    linear_cost,
    price,
    anchor,
    hessian,
    usage_coef,
    crew_limit,
    crew_dual,
    crew_row,
    bundle_of,
    scen_weight,
):
    count, vehicles, n = start_plan.shape
    crews = crew_limit.shape[1]
    bundle_count = anchor.shape[0]
    me = lax.axis_index("scen")
    all_bundles = bundle_of[:, 0]
    my_bundles = lax.dynamic_slice_in_dim(all_bundles, me * count, count)
    all_weights = scen_weight.astype(f32)
    my_weights = lax.dynamic_slice_in_dim(all_weights, me * count, count)

    pad = ((0, 0), (0, CREW_PAD - crews))
    limit = jnp.pad(crew_limit, pad)
    dual = jnp.pad(crew_dual, pad)
    def per_scen(*shape):
        return pl.BlockSpec((1, *shape), lambda s, *_: (s, 0, 0))

    def whole(*shape):
        return pl.BlockSpec(shape, lambda s, *_: (0,) * len(shape))

    params = pltpu.CompilerParams(
        dimension_semantics=("arbitrary",), vmem_limit_bytes=LIMIT
    )
    tall = pltpu.VMEM((count, n, vehicles), f32)
    flat_block = per_scen(vehicles, n)
    pair_block = pl.BlockSpec((2, vehicles, n), lambda s, *_: (s, 0, 0))
    vm = vmem_spec()

    partial, linear, coef_t, row_to_veh, usage = pl.pallas_call(
        first_kernel,
        grid_spec=pltpu.PrefetchScalarGridSpec(
            num_scalar_prefetch=1,
            grid=(count // 2,),
            in_specs=[
                pair_block,
                pair_block,
                pair_block,
                pl.BlockSpec((1, vehicles, n), lambda s, b: (b[2 * s], 0, 0)),
                pl.BlockSpec((1, vehicles, n), lambda s, b: (b[2 * s + 1], 0, 0)),
                pl.BlockSpec((2, n, n), lambda s, *_: (s, 0, 0)),
                whole(vehicles, n),
                whole(count, crews),
                whole(1, vehicles),
            ],
            out_specs=[vm] * 5,
            scratch_shapes=[
                pltpu.VMEM((16, 1, vehicles), f32),
                pltpu.VMEM((56, 8, vehicles), f32),
                pltpu.VMEM((2 * n, 2 * n), bf16),
                pltpu.VMEM((count, CREW_PAD), f32),
            ],
        ),
        out_shape=[
            tall,
            tall,
            pltpu.VMEM((n, vehicles), f32),
            pltpu.VMEM((CREW_PAD, vehicles), bf16),
            pltpu.VMEM((56, CREW_PAD), f32),
        ],
        compiler_params=params,
        name="first_steps",
    )(
        my_bundles,
        in_hbm(start_plan),
        in_hbm(linear_cost),
        in_hbm(price),
        in_hbm(anchor),
        in_hbm(anchor),
        in_hbm(hessian),
        in_hbm(usage_coef),
        crew_dual,
        crew_row[None, :],
    )

    use = usage_exchange(usage)
    norms = summed(*[u[48:56] for u in use])
    for _ in range(3):
        partial, usage, dual = pl.pallas_call(
            middle_kernel,
            in_specs=[vm] * 12,
            out_specs=[vm] * 3,
            out_shape=[
                tall,
                pltpu.VMEM((48, CREW_PAD), f32),
                pltpu.VMEM((count, CREW_PAD), f32),
            ],
            input_output_aliases={0: 0},
            scratch_shapes=[
                pltpu.VMEM((48, 1, vehicles), f32),
                pltpu.VMEM((48, 8, vehicles), f32),
                pltpu.VMEM((2 * n, 2 * n), bf16),
            ],
            compiler_params=pltpu.CompilerParams(vmem_limit_bytes=LIMIT),
            name="three_steps",
        )(
            *[
                in_vmem(a)
                for a in (
                    partial,
                    linear,
                    hessian,
                    coef_t,
                    *use,
                    norms,
                    limit,
                    dual,
                    row_to_veh,
                )
            ]
        )
        use = usage_exchange(usage)

    me_y, me_x = np.arange(16)[:, None] // 4, np.arange(16)[:, None] % 4
    it_y, it_x = np.arange(16)[None, :] // 4, np.arange(16)[None, :] % 4
    place_a = ((it_x - me_x) % 4) * 4 + (it_y - me_y) % 4
    place_b = ((it_y - me_y) % 4) * 4 + (it_x - me_x) % 4
    here = jnp.arange(16, dtype=jnp.int32) == me
    row_a = jnp.sum(jnp.where(here[:, None], place_a, 0), axis=0)
    row_b = jnp.sum(jnp.where(here[:, None], place_b, 0), axis=0)
    ids = jnp.arange(16, dtype=jnp.int32)
    hot = my_bundles[:, None] == ids[None, :]
    slots = jnp.stack(
        [jnp.sum(jnp.where(hot, row[None, :], 0), axis=1) for row in (row_a, row_b)]
    ).astype(jnp.int32)
    same = my_bundles[:, None] == my_bundles[None, :]
    before = jnp.arange(count)[None, :] < jnp.arange(count)[:, None]
    held = jnp.sum(jnp.where(same & before, my_weights[None, :], 0.0), axis=1)
    factors = jnp.stack(
        [
            my_weights,
            held * my_weights / (held + my_weights),
            1.0 / jnp.maximum(held, 1.0),
        ]
    )
    half = vehicles // 2
    bundle_sums = pltpu.VMEM((bundle_count, half, n), f32)
    quarter = pltpu.VMEM((4, half // 2, n), f32)
    plan, roster, sum_a, sum_b, up_a, down_a, up_b, down_b, spread, dual = pl.pallas_call(
        last_kernel,
        grid_spec=pltpu.PrefetchScalarGridSpec(
            num_scalar_prefetch=2,
            grid=(count,),
            in_specs=[vm] * 12,
            out_specs=[flat_block] + [vm] * 9,
            scratch_shapes=[pltpu.VMEM((32, 1, vehicles), f32)],
        ),
        out_shape=[
            jax.ShapeDtypeStruct((count, vehicles, n), bf16),
            pltpu.VMEM((count, vehicles, n), f32),
            bundle_sums,
            bundle_sums,
            quarter,
            quarter,
            quarter,
            quarter,
            pltpu.VMEM((8, n), f32),
            pltpu.VMEM((count, CREW_PAD), f32),
        ],
        compiler_params=params,
        name="last_step",
    )(
        slots,
        factors,
        *[
            in_vmem(a)
            for a in (
                partial,
                linear,
                hessian,
                coef_t,
                *use,
                norms,
                limit,
                dual,
                row_to_veh,
            )
        ],
    )

    owners = jnp.arange(all_bundles.shape[0], dtype=jnp.int32) // count

    def weight_table(row):
        device = jnp.sum(jnp.where(owners[:, None] == ids[None, :], row[None, :], 0), axis=1)
        bundle = jnp.sum(jnp.where(all_bundles[:, None] == ids[None, :], row[None, :], 0), axis=1)
        return jnp.sum(
            jnp.where(
                (device[None, None, :] == ids[:, None, None])
                & (bundle[None, None, :] == ids[None, :, None]),
                all_weights[None, None, :],
                0.0,
            ),
            axis=2,
        )

    weights_a = weight_table(row_a)
    weights_b = weight_table(row_b)

    sides = (
        ("x", "y", weights_a, sum_a, up_a, down_a),
        ("y", "x", weights_b, sum_b, up_b, down_b),
    )
    flow = (2, 4, half // 2, n)
    flat = (half, n)
    moved = [(shift(up, f, 1), shift(down, f, -1)) for f, _, _, _, up, down in sides]
    moved = [
        local_call(forward_kernel, w, (sums, up, down), [flow, flow], "forward")
        for (_, _, w, sums, _, _), (up, down) in zip(sides, moved)
    ]
    spreads = [spread] + [m[2] for m in moved]
    moved = [(shift(m[0], side[0], 1), shift(m[1], side[0], -1)) for side, m in zip(sides, moved)]
    moved = [
        local_call(arrive_kernel, w, (sums, up, down), [flat] * 4, "arrive")
        for (_, _, w, sums, _, _), (up, down) in zip(sides, moved)
    ]
    spreads += [m[4] for m in moved]
    moved = [
        (m[0], *[shift(m[by], side[1], by) for by in (1, 2, 3)]) for side, m in zip(sides, moved)
    ]
    own_b, spread = local_call(finish_kernel, sides[1][2], moved[1], [flat], "finish")
    own_a = local_call(
        finish_last_kernel, sides[0][2], (*moved[0], *spreads, spread), [(half + 8, n)], "finish"
    )[0]
    row_a, row_b = gather_row(own_a, "y"), gather_row(own_b, "x")
    spread = summed(*[row_a[k][half:] for k in range(4)])
    row_a = {k: row_a[k][:half] for k in range(4)}
    pack_a, pack_b = gather_pack(row_a), gather_pack(row_b)
    pack_a, pack_b, spread = lax.optimization_barrier((pack_a, pack_b, spread))
    near_a, near_b = gather_near(pack_a, "x"), gather_near(pack_b, "y")
    spread = spread_over_veh(spread)
    spread_total = spread_over_x(spread)
    means = gather_far(*near_a, "x") + gather_far(*near_b, "y")
    entries = vehicles * lax.axis_size("veh") * n

    each = 4
    four_block = pl.BlockSpec((each, vehicles, n), lambda s, *_: (s, 0, 0))
    new_price, gap = pl.pallas_call(
        price_kernel,
        grid_spec=pltpu.PrefetchScalarGridSpec(
            num_scalar_prefetch=1,
            grid=(count // each,),
            in_specs=[vm, four_block] + [vm] * 12,
            out_specs=[four_block, whole(1, 1)],
        ),
        out_shape=[
            jax.ShapeDtypeStruct((count, vehicles, n), bf16),
            jax.ShapeDtypeStruct((1, 1), f32),
        ],
        compiler_params=params,
        name="new_price",
    )(
        slots,
        in_vmem(roster),
        in_hbm(price),
        in_vmem(spread_total),
        in_vmem((all_weights * entries)[None, :]),
        *[in_vmem(m) for m in means],
    )

    own_mean = jnp.concatenate([own_a[:half], own_b], axis=0)
    return (plan, new_price, own_mean.astype(bf16)[None], dual[:, :crews], gap[0, 0])


def solution(mesh):
    return jax.shard_map(
        shards,
        mesh=mesh,
        in_specs=(
            P("scen", "veh", None),
            P("scen", "veh", None),
            P("scen", "veh", None),
            P(None, "veh", None),
            P("scen", None, None),
            P("veh", None),
            P("scen", None),
            P("scen", None),
            P("veh"),
            P(),
            P(),
        ),
        out_specs=(
            P("scen", "veh", None),
            P("scen", "veh", None),
            P("scen", "veh", None),
            P("scen", None),
            P(),
        ),
        check_vma=False,
    )
```
